32 devices in a mesh: dp: 8 (over z, x), mp: 4 (over y, core).
Axes of the slice: x: 2, y: 2, z: 4, core: 2. Of those that a mesh axis runs over, the one named last changes fastest.
Arguments:
- attn: bfloat16 [2, 512, 2048], P(None, 'dp', 'mp'), may hold values from -6 to 6
- resid: bfloat16 [2, 512, 4096], P(None, 'dp', 'mp'), may hold values from -6 to 6
- w_out: bfloat16 [4096, 2048], P('dp', 'mp'), may hold values from -0.125 to 0.125
- gain: float32 [4096], P('mp'), may hold values from 0.1 to 1.9
- neg_owner: int32 [512, 31], P('dp'), may hold values from 0 to 7, as said below
- neg_local: int32 [512, 31], P('dp'), may hold values from 0 to 63
Outputs:
- attn_grad: bfloat16 [2, 512, 2048], P(None, 'dp', 'mp')
- weight_grad: float32 [4096, 2048], P('dp', 'mp')
- gain_grad: float32 [4096], P('mp')
The draws below stay inside these ranges and needn't reach their ends.
Inputs may be any that keep to these rules, and one draw needn't show every extreme that they name: `neg_owner`: among the 64 queries of one index of dp (aligned blocks of rows), no owner is named more than 496 times, and some owner exactly 496 times.
All inputs are finite; a program needn't handle non-finite values.
Results may differ from the reference program's by a relative error of at most 0.0052.
Values may be sent and summed in bfloat16 or wider, within the bound.
A program may use at most 128 MiB of HBM per device.

```python
import jax
import jax.numpy as jnp
from jax import lax

D = 4096
HD = 2048
NEG = 31
PAIRS_DEV = 64
PAIRS = 512
CAP = 496
N_DP = 8


def draw_neg_owner(key, part):
    keys = jax.random.split(key, N_DP)
    total = N_DP * CAP

    def one_block(block_key):
        key_hot, key_order, key_shuffle = jax.random.split(block_key, 3)
        hot = jax.random.randint(key_hot, (), 0, N_DP)
        slots = jnp.arange(total, dtype=jnp.int32)
        owner = slots // CAP
        order = jax.random.permutation(key_order, total).astype(jnp.int32)
        position = jnp.zeros((total,), jnp.int32).at[order].set(slots)
        ranking = jnp.where(owner == hot, slots - total, position)
        chosen = jnp.argsort(ranking)[:PAIRS_DEV * NEG]
        picked = jax.random.permutation(key_shuffle, owner[chosen])
        return picked.reshape(PAIRS_DEV, NEG)
    return jax.vmap(one_block)(keys).reshape(PAIRS_DEV * N_DP, NEG).astype(jnp.int32)


def set_ends(entries, own_key, least, high):
    index_at = [jax.random.randint(jax.random.fold_in(own_key, axis), (), 0, length) for axis, length in enumerate(entries.shape)]
    longest = entries.shape.index(max(entries.shape))
    next_to = index_at[:longest] + [(index_at[longest] + 1) % entries.shape[longest]] + index_at[longest + 1:]
    return entries.at[tuple(index_at)].set(least).at[tuple(next_to)].set(high)


def shard_levels(own_key, dims, cuts, low, top_value):
    def one(axis_at, parts):
        draws = jax.random.uniform(jax.random.fold_in(jax.random.fold_in(own_key, 6), axis_at), (parts,), jnp.float32, low / len(cuts), top_value / len(cuts))
        return jnp.repeat(jnp.exp(draws), dims[axis_at] // parts).reshape((-1,) + (1,) * (len(dims) - axis_at - 1))

    loudness = one(*cuts[0])
    for cut in cuts[1:]:
        loudness = loudness * one(*cut)
    return loudness


def noise(stream_key, extent, spread, bound, pieces=(), kind=jnp.bfloat16):
    entries = jax.random.normal(stream_key, extent, jnp.float32) * spread
    if len(pieces) > 0:
        entries = shard_levels(stream_key, extent, pieces, -0.22, 0.18) * entries
    return jnp.clip(entries, min=-bound, max=bound).astype(kind)


def setup_inputs(seed: int = 0) -> dict:
    streams_of = jax.random.split(jax.random.key(seed), 7)
    attn = noise(streams_of[0], (2, PAIRS, HD), 1.0, 6.0, ((1, 8), (2, 4)))
    resid = noise(streams_of[1], (2, PAIRS, D), 1.0, 6.0, ((1, 8), (2, 4)))
    w_out = noise(streams_of[2], (D, HD), HD ** -0.5, 0.125, ((0, 8), (1, 4)))
    gain = jnp.clip(1.0 + 0.18 * jax.random.normal(streams_of[3], (D,), jnp.float32), 0.1, 1.9)
    neg_owner = draw_neg_owner(jax.random.fold_in(streams_of[6], 71), 0)
    neg_local = set_ends(jax.random.randint(streams_of[5], (PAIRS, NEG), 0, PAIRS_DEV), jax.random.fold_in(streams_of[5], 1), 0, PAIRS_DEV - 1).astype(jnp.int32)
    return dict(attn=attn, resid=resid, w_out=w_out, gain=gain, neg_owner=neg_owner, neg_local=neg_local)


TAU = 0.05
LOSS_SCALE = 32.0
EPS = 1e-06

def reference(attn, resid, w_out, gain, neg_owner, neg_local):
    rows_a = attn.reshape(2 * PAIRS, HD)
    proj = jnp.dot(rows_a, w_out.T, preferred_element_type=jnp.float32)
    hidden = resid.reshape(2 * PAIRS, D).astype(jnp.float32) + proj
    normed = hidden * gain
    recip = lax.rsqrt(lax.optimization_barrier(jnp.sum(normed * normed, axis=1, keepdims=True)) + EPS)
    emb = (normed * recip).astype(jnp.bfloat16)
    query = emb[:PAIRS].astype(jnp.float32)
    docs = emb[PAIRS:].astype(jnp.float32)
    doc_ids = (neg_owner * PAIRS_DEV + neg_local).astype(jnp.int32)
    ids_t = jnp.transpose(doc_ids)
    pos_score = lax.optimization_barrier(jnp.sum(query * docs, axis=1)) / TAU

    def neg_score(ids):
        return lax.optimization_barrier(jnp.sum(query * docs[ids], axis=1)) / TAU
    neg_scores = jnp.transpose(lax.map(neg_score, ids_t))
    scores = jnp.concatenate([pos_score[:, None], neg_scores], axis=1)
    expo = jnp.exp(scores)
    prob = expo / lax.optimization_barrier(jnp.sum(expo, axis=1, keepdims=True))
    first = (jnp.arange(NEG + 1) == 0).astype(jnp.float32)[None, :]
    wts = LOSS_SCALE * (prob - first) / TAU

    def accum(carry, inputs):
        dq_acc, dd_acc = carry
        ids, wcol = inputs
        dq_acc = dq_acc + wcol[:, None] * docs[ids]
        term = (wcol[:, None] * query).astype(jnp.bfloat16).astype(jnp.float32)
        dd_acc = dd_acc + jax.ops.segment_sum(term, ids, num_segments=PAIRS)
        return ((dq_acc, dd_acc), None)
    start = (wts[:, 0:1] * docs, wts[:, 0:1] * query)
    (dq, dd), _ = lax.scan(accum, start, (ids_t, jnp.transpose(wts[:, 1:])))
    demb = jnp.concatenate([dq, dd], axis=0)
    inner = lax.optimization_barrier(jnp.sum(normed * demb, axis=1, keepdims=True))
    dnorm = recip * demb - recip * recip * recip * normed * inner
    gain_grad = lax.optimization_barrier(jnp.sum(dnorm * hidden, axis=0))
    dh = (dnorm * gain).astype(jnp.bfloat16)
    attn_grad = jnp.dot(dh, w_out, preferred_element_type=jnp.float32).astype(jnp.bfloat16).reshape(2, PAIRS, HD)
    weight_grad = jnp.dot(dh.T, rows_a, preferred_element_type=jnp.float32)
    return (attn_grad, weight_grad, gain_grad)
```

```python
import jax
import jax.numpy as jnp
from jax import lax
from jax.sharding import PartitionSpec as P

TAU = 0.05
LOSS_SCALE = 32.0
EPS = 1e-06


def by_query(attn, resid, w_out, gain, neg_owner, neg_local):
    groups = lax.axis_size("dp")
    pairs_here = attn.shape[1]
    feats = resid.shape[2]
    neg_count = neg_owner.shape[1]
    capacity = 2 * pairs_here * neg_count // groups
    rows_a = attn.reshape(2 * pairs_here, attn.shape[2])
    weight_full = lax.all_gather(w_out, "dp", axis=0, tiled=True)
    proj_part = lax.dot_general(
        rows_a, weight_full, (((1,), (1,)), ((), ())), preferred_element_type=jnp.float32
    )
    proj = lax.psum_scatter(proj_part, "mp", scatter_dimension=1, tiled=True)
    hidden = resid.reshape(2 * pairs_here, feats).astype(jnp.float32) + proj
    normed = hidden * gain
    squares = lax.psum(jnp.sum(normed * normed, axis=1), "mp")
    recip = lax.rsqrt(squares + EPS)[:, None]
    emb = (normed * recip).astype(jnp.bfloat16)
    query = emb[:pairs_here]
    docs = emb[pairs_here:]
    flat_owner = neg_owner.reshape(-1)
    flat_local = neg_local.reshape(-1)
    onehot = (flat_owner[:, None] == jnp.arange(groups, dtype=jnp.int32)[None, :]).astype(jnp.int32)
    ranks = jnp.sum((jnp.cumsum(onehot, axis=0) - 1) * onehot, axis=1)
    slot = flat_owner * capacity + ranks
    request = jnp.full((groups * capacity,), -1, jnp.int32).at[slot].set(flat_local)
    asked = lax.all_to_all(
        request.reshape(groups, capacity), "dp", split_axis=0, concat_axis=0, tiled=True
    )
    valid = asked >= 0
    safe_rows = jnp.maximum(asked, 0)
    outgoing = jnp.where(valid[:, :, None], docs[safe_rows], jnp.zeros((), jnp.bfloat16))
    fetched = lax.all_to_all(outgoing, "dp", split_axis=0, concat_axis=0, tiled=True)
    neg_emb = fetched.reshape(groups * capacity, feats)[slot].reshape(pairs_here, neg_count, feats)
    pos_part = jnp.sum(query.astype(jnp.float32) * docs.astype(jnp.float32), axis=1)
    neg_part = jnp.einsum("pd,pkd->pk", query, neg_emb, preferred_element_type=jnp.float32)
    partial_value = jnp.concatenate([pos_part[:, None], neg_part], axis=1)
    scores = lax.psum(partial_value, "mp") / TAU
    expo = jnp.exp(scores)
    prob = expo / jnp.sum(expo, axis=1, keepdims=True)
    first = (jnp.arange(neg_count + 1) == 0).astype(jnp.float32)[None, :]
    wts = LOSS_SCALE * (prob - first) / TAU
    query_f = query.astype(jnp.float32)
    grad_query = wts[:, 0:1] * docs.astype(jnp.float32) + jnp.einsum(
        "pk,pkd->pd", wts[:, 1:], neg_emb, preferred_element_type=jnp.float32
    )
    terms = (wts[:, 1:, None] * query_f[:, None, :]).astype(jnp.bfloat16)
    slot_buffer = (
        jnp.zeros((groups * capacity, feats), jnp.bfloat16).at[slot].set(terms.reshape(-1, feats))
    )
    returned = lax.all_to_all(
        slot_buffer.reshape(groups, capacity, feats), "dp", split_axis=0, concat_axis=0, tiled=True
    )
    targets = jnp.where(valid, asked, pairs_here).reshape(-1)
    selector = (jnp.arange(pairs_here, dtype=jnp.int32)[:, None] == targets[None, :]).astype(
        jnp.bfloat16
    )
    grad_docs = wts[:, 0:1] * query_f + jnp.dot(
        selector, returned.reshape(-1, feats), preferred_element_type=jnp.float32
    )
    demb = jnp.concatenate([grad_query, grad_docs], axis=0)
    inner = lax.psum(jnp.sum(normed * demb, axis=1), "mp")[:, None]
    dnorm = recip * demb - recip * recip * recip * normed * inner
    gain_grad = lax.psum(jnp.sum(dnorm * hidden, axis=0), "dp")
    dh = (dnorm * gain).astype(jnp.bfloat16)
    dh_full = lax.all_gather(dh, "mp", axis=1, tiled=True)
    attn_grad = (
        jnp.dot(dh_full, weight_full, preferred_element_type=jnp.float32)
        .astype(jnp.bfloat16)
        .reshape(attn.shape)
    )
    weight_grad = lax.psum_scatter(
        lax.dot_general(
            dh_full, rows_a, (((0,), (0,)), ((), ())), preferred_element_type=jnp.float32
        ),
        "dp",
        scatter_dimension=0,
        tiled=True,
    )
    return (attn_grad, weight_grad, gain_grad)


def by_feature(attn, resid, w_out, gain, neg_owner, neg_local):
    groups, quarters = lax.axis_size("dp"), lax.axis_size("mp")
    d, m = lax.axis_index("dp"), lax.axis_index("mp")
    pairs_here = attn.shape[1]
    rows_here = 2 * pairs_here
    pairs = groups * pairs_here
    heads = attn.shape[2]
    feats = resid.shape[2]
    block = w_out.shape[0] // quarters
    per = feats // (block * quarters)
    place = d * quarters + m

    rows_a = lax.all_gather(attn.reshape(rows_here, heads), "dp", axis=0, tiled=True)
    moved = lax.all_to_all(
        resid.reshape(rows_here, per, quarters, block), "mp", split_axis=2, concat_axis=2, tiled=True
    )
    moved = moved.transpose(2, 1, 0, 3).reshape(groups, rows_here, block)
    moved = lax.all_to_all(moved, "dp", split_axis=0, concat_axis=0, tiled=True)
    gain_all = lax.all_gather(gain, "mp", axis=0, tiled=True)
    gain_here = lax.dynamic_slice(gain_all, (place * block,), (block,))

    proj_part = lax.dot_general(
        rows_a, w_out, (((1,), (1,)), ((), ())), preferred_element_type=jnp.float32
    )
    proj = lax.psum_scatter(proj_part, "mp", scatter_dimension=1, tiled=True)
    hidden = moved.reshape(groups * rows_here, block).astype(jnp.float32) + proj
    normed = hidden * gain_here
    split = (groups, 2, pairs_here, block)
    rough = normed.astype(jnp.bfloat16).reshape(split)
    dots_part = lax.dot_general(
        rough[:, 0].reshape(pairs, block),
        rough[:, 1].reshape(pairs, block),
        (((1,), (1,)), ((), ())),
        preferred_element_type=jnp.float32,
    )
    dots = lax.psum_scatter(dots_part, ("dp", "mp"), scatter_dimension=0, tiled=True)
    squares = lax.psum(jnp.sum(normed * normed, axis=1), ("dp", "mp"))
    recip = lax.rsqrt(squares + EPS)
    recip_split = recip.reshape(groups, 2, pairs_here)

    queries = pairs // (groups * quarters)
    recip_q = lax.dynamic_slice(recip_split[:, 0].reshape(pairs), (place * queries,), (queries,))
    recip_e = recip_split[:, 1].reshape(pairs)
    cosine = dots * recip_q[:, None] * recip_e[None, :]
    ids = neg_owner * pairs_here + neg_local
    ids = lax.dynamic_slice(ids, (m * queries, 0), (queries, ids.shape[1]))
    column = jnp.arange(pairs, dtype=jnp.int32)
    own = (place * queries + jnp.arange(queries, dtype=jnp.int32))[:, None] == column[None, :]
    own = own.astype(jnp.float32)
    times = own + jnp.sum((ids[:, :, None] == column).astype(jnp.float32), axis=1)
    expo = times * jnp.exp(cosine / TAU)
    prob = expo / jnp.sum(expo, axis=1, keepdims=True)
    wts = LOSS_SCALE * (prob - own) / TAU
    along = wts * cosine
    along_q = jnp.pad(jnp.sum(along, axis=1)[None, :], ((0, 0), (0, pairs - queries)))
    along_e = jnp.sum(along, axis=0)[None, :]
    packed = jnp.concatenate([wts, along_q, along_e], axis=0)
    packed = jnp.pad(packed, ((0, -packed.shape[0] % 8), (0, 0)))
    packed = lax.all_gather(packed, ("dp", "mp"), axis=0)
    wts_all = packed[:, :queries].reshape(pairs, pairs).astype(jnp.bfloat16)
    along_q = packed[:, queries, :queries].reshape(groups, 1, pairs_here)
    along_e = jnp.sum(packed[:, queries + 1], axis=0).reshape(groups, 1, pairs_here)
    along_all = jnp.concatenate([along_q, along_e], axis=1).reshape(-1, 1)

    recip = recip[:, None]
    unit = normed * recip
    emb = unit.astype(jnp.bfloat16).reshape(split)
    grad_q = jnp.dot(
        wts_all, emb[:, 1].reshape(pairs, block), preferred_element_type=jnp.float32
    )
    grad_e = lax.dot_general(
        wts_all,
        emb[:, 0].reshape(pairs, block),
        (((0,), (0,)), ((), ())),
        preferred_element_type=jnp.float32,
    )
    one = (groups, 1, pairs_here, block)
    demb = jnp.concatenate([grad_q.reshape(one), grad_e.reshape(one)], axis=1).reshape(-1, block)
    dnorm = recip * (demb - unit * along_all)
    gain_grad = lax.all_gather(jnp.sum(dnorm * hidden, axis=0), ("dp", "mp"), axis=0, tiled=True)
    gain_grad = lax.dynamic_slice(gain_grad, (m * feats,), (feats,))
    dh = (dnorm * gain_here).astype(jnp.bfloat16)
    dh_full = lax.all_gather(dh, "mp", axis=1, tiled=True)
    attn_part = jnp.dot(dh_full, w_out, preferred_element_type=jnp.float32)
    attn_grad = lax.psum_scatter(attn_part, "dp", scatter_dimension=0, tiled=True)
    attn_grad = attn_grad.astype(jnp.bfloat16).reshape(attn.shape)
    weight_grad = lax.dot_general(
        dh_full, rows_a, (((0,), (0,)), ((), ())), preferred_element_type=jnp.float32
    )
    return (attn_grad, weight_grad, gain_grad)


def shards(attn, resid, w_out, gain, neg_owner, neg_local):
    groups, quarters = lax.axis_size("dp"), lax.axis_size("mp")
    block = w_out.shape[0] // quarters
    fits = block % 128 == 0 and resid.shape[2] % (block * quarters) == 0
    fits = fits and groups * attn.shape[1] <= 1024 and attn.shape[1] % quarters == 0
    plan = by_feature if fits else by_query
    return plan(attn, resid, w_out, gain, neg_owner, neg_local)


def solution(mesh):
    in_specs = (
        P(None, "dp", "mp"),
        P(None, "dp", "mp"),
        P("dp", "mp"),
        P("mp"),
        P("dp", None),
        P("dp", None),
    )
    out_specs = (P(None, "dp", "mp"), P("dp", "mp"), P("mp"))
    return jax.shard_map(shards, mesh=mesh, in_specs=in_specs, out_specs=out_specs, check_vma=False)
```

```python
import functools

import jax
import jax.numpy as jnp
from jax import lax
from jax.experimental import pallas as pl
from jax.experimental.pallas import tpu as pltpu
from jax.sharding import PartitionSpec as P

TAU = 0.05
LOSS_SCALE = 32.0
EPS = 1e-06


def by_query(attn, resid, w_out, gain, neg_owner, neg_local):
    groups = lax.axis_size("dp")
    pairs_here = attn.shape[1]
    feats = resid.shape[2]
    neg_count = neg_owner.shape[1]
    capacity = 2 * pairs_here * neg_count // groups
    rows_a = attn.reshape(2 * pairs_here, attn.shape[2])
    weight_full = lax.all_gather(w_out, "dp", axis=0, tiled=True)
    proj_part = lax.dot_general(
        rows_a, weight_full, (((1,), (1,)), ((), ())), preferred_element_type=jnp.float32
    )
    proj = lax.psum_scatter(proj_part, "mp", scatter_dimension=1, tiled=True)
    hidden = resid.reshape(2 * pairs_here, feats).astype(jnp.float32) + proj
    normed = hidden * gain
    squares = lax.psum(jnp.sum(normed * normed, axis=1), "mp")
    recip = lax.rsqrt(squares + EPS)[:, None]
    emb = (normed * recip).astype(jnp.bfloat16)
    query = emb[:pairs_here]
    docs = emb[pairs_here:]
    flat_owner = neg_owner.reshape(-1)
    flat_local = neg_local.reshape(-1)
    onehot = (flat_owner[:, None] == jnp.arange(groups, dtype=jnp.int32)[None, :]).astype(jnp.int32)
    ranks = jnp.sum((jnp.cumsum(onehot, axis=0) - 1) * onehot, axis=1)
    slot = flat_owner * capacity + ranks
    request = jnp.full((groups * capacity,), -1, jnp.int32).at[slot].set(flat_local)
    asked = lax.all_to_all(
        request.reshape(groups, capacity), "dp", split_axis=0, concat_axis=0, tiled=True
    )
    valid = asked >= 0
    safe_rows = jnp.maximum(asked, 0)
    outgoing = jnp.where(valid[:, :, None], docs[safe_rows], jnp.zeros((), jnp.bfloat16))
    fetched = lax.all_to_all(outgoing, "dp", split_axis=0, concat_axis=0, tiled=True)
    neg_emb = fetched.reshape(groups * capacity, feats)[slot].reshape(pairs_here, neg_count, feats)
    pos_part = jnp.sum(query.astype(jnp.float32) * docs.astype(jnp.float32), axis=1)
    neg_part = jnp.einsum("pd,pkd->pk", query, neg_emb, preferred_element_type=jnp.float32)
    partial_value = jnp.concatenate([pos_part[:, None], neg_part], axis=1)
    scores = lax.psum(partial_value, "mp") / TAU
    expo = jnp.exp(scores)
    prob = expo / jnp.sum(expo, axis=1, keepdims=True)
    first = (jnp.arange(neg_count + 1) == 0).astype(jnp.float32)[None, :]
    wts = LOSS_SCALE * (prob - first) / TAU
    query_f = query.astype(jnp.float32)
    grad_query = wts[:, 0:1] * docs.astype(jnp.float32) + jnp.einsum(
        "pk,pkd->pd", wts[:, 1:], neg_emb, preferred_element_type=jnp.float32
    )
    terms = (wts[:, 1:, None] * query_f[:, None, :]).astype(jnp.bfloat16)
    slot_buffer = (
        jnp.zeros((groups * capacity, feats), jnp.bfloat16).at[slot].set(terms.reshape(-1, feats))
    )
    returned = lax.all_to_all(
        slot_buffer.reshape(groups, capacity, feats), "dp", split_axis=0, concat_axis=0, tiled=True
    )
    targets = jnp.where(valid, asked, pairs_here).reshape(-1)
    selector = (jnp.arange(pairs_here, dtype=jnp.int32)[:, None] == targets[None, :]).astype(
        jnp.bfloat16
    )
    grad_docs = wts[:, 0:1] * query_f + jnp.dot(
        selector, returned.reshape(-1, feats), preferred_element_type=jnp.float32
    )
    demb = jnp.concatenate([grad_query, grad_docs], axis=0)
    inner = lax.psum(jnp.sum(normed * demb, axis=1), "mp")[:, None]
    dnorm = recip * demb - recip * recip * recip * normed * inner
    gain_grad = lax.psum(jnp.sum(dnorm * hidden, axis=0), "dp")
    dh = (dnorm * gain).astype(jnp.bfloat16)
    dh_full = lax.all_gather(dh, "mp", axis=1, tiled=True)
    attn_grad = (
        jnp.dot(dh_full, weight_full, preferred_element_type=jnp.float32)
        .astype(jnp.bfloat16)
        .reshape(attn.shape)
    )
    weight_grad = lax.psum_scatter(
        lax.dot_general(
            dh_full, rows_a, (((0,), (0,)), ((), ())), preferred_element_type=jnp.float32
        ),
        "dp",
        scatter_dimension=0,
        tiled=True,
    )
    return (attn_grad, weight_grad, gain_grad)


MESH = pl.DeviceIdType.MESH
BF = jnp.bfloat16
F32 = jnp.float32


def matmul(left, right, left_dim, right_dim, precision=None):
    return lax.dot_general(
        left,
        right,
        (((left_dim,), (right_dim,)), ((), ())),
        precision=precision,
        preferred_element_type=F32,
    )


def fused(
    groups,
    quarters,
    attn,
    resid,
    w_out,
    gain,
    owner,
    local,
    attn_grad,
    weight_grad,
    gain_grad,
    rows_a,
    res_all,
    gain_all,
    proj_out,
    proj_in,
    sq,
    dots_out,
    dots_in,
    wts_in,
    extra_in,
    scale,
    gg,
    dh,
    xpart,
    xin,
    zpart,
    zin,
    zsend,
    xsend,
    arecv,
    rsend,
    rrecv,
    gsend,
    grecv,
    psend,
    precv,
    allsend,
    allrecv,
    hsend,
    hrecv,
    xsend2,
    xrecv2,
    zsend2,
    zrecv2,
):
    d, m = lax.axis_index("dp"), lax.axis_index("mp")
    total = groups * quarters
    me = d * quarters + m
    here = attn.shape[1]
    pairs = groups * here
    block = w_out.shape[0] // quarters
    own_rows = pairs // total
    zc, xc = d // 2, d % 2
    depth = groups // 2
    partner = zc * 2 + (1 - xc)

    def at_dp(t):
        return (t, m)

    def at_mp(t):
        return (d, t)

    def at_any(t):
        return (t // quarters, t % quarters)

    def send(src, dst, s, r, dev):
        return pltpu.make_async_remote_copy(
            src_ref=src, dst_ref=dst, send_sem=s, recv_sem=r, device_id=dev, device_id_type=MESH
        )

    def grp(s):
        return pl.ds(pl.multiple_of(s * here, here), here)

    def others(k):
        return lax.rem(me + k, total)

    barrier = pltpu.get_barrier_semaphore()

    def greet(k, c):
        pl.semaphore_signal(barrier, inc=1, device_id=at_any(others(k)), device_id_type=MESH)
        return c

    lax.fori_loop(1, total, greet, 0)
    pl.semaphore_wait(barrier, total - 1)

    pending = []
    first = send(attn, rows_a.at[:, grp(d), :], xsend.at[0], arecv.at[d], at_dp(partner))
    first.start()
    pending.append(first)
    for k in range(1, depth):
        t = lax.rem(zc + k, depth) * 2 + xc
        c = send(attn, rows_a.at[:, grp(d), :], zsend.at[k - 1], arecv.at[d], at_dp(t))
        c.start()
        pending.append(c)
    for k in range(1, quarters):
        c = send(gain, gain_all.at[m], gsend.at[k - 1], grecv.at[m], at_mp(lax.rem(m + k, quarters)))
        c.start()
        pending.append(c)
    gain_all[m] = gain[...]

    res_sends = []
    for a in range(2):
        for j in range(quarters):
            cols = pl.ds((a * quarters + j) * block, block)
            td = 2 * m + a
            is_self = jnp.logical_and(td == d, m == j)
            c = send(
                resid.at[:, :, cols],
                res_all.at[:, grp(d), :],
                rsend.at[a * quarters + j],
                rrecv.at[d],
                (td, jnp.int32(j)),
            )
            res_sends.append((is_self, c))

            @pl.when(jnp.logical_not(is_self))
            def _(c=c):
                c.start()

            @pl.when(is_self)
            def _(cols=cols):
                res_all[:, grp(d), :] = resid[:, :, cols]

    def project(s, i):
        part = matmul(rows_a[:, grp(s), :].reshape(2 * here, -1), w_out[...], 1, 1)
        for j in range(quarters):
            piece = part[:, j * block : (j + 1) * block].astype(BF)
            proj_out[j, :, grp(s), :] = piece.reshape(2, here, block)
        for k in range(1, quarters):
            t = lax.rem(m + k, quarters)
            c = send(
                proj_out.at[t, :, grp(s), :],
                proj_in.at[m, :, grp(s), :],
                psend.at[k - 1, i],
                precv.at[m, s],
                at_mp(t),
            )
            c.start()
            pending.append(c)

    def wait_rows(s):
        send(attn, rows_a.at[:, grp(s), :], zsend.at[0], arecv.at[s], at_dp(partner)).wait_recv()

    rows_a[:, grp(d), :] = attn[...]
    project(d, 0)
    for k in range(1, depth):
        s = lax.rem(zc + depth - k, depth) * 2 + xc
        wait_rows(s)
        slot = rows_a.at[:, grp(s), :]
        c = send(slot, slot, xsend.at[k], arecv.at[s], at_dp(partner))
        c.start()
        pending.append(c)
        project(s, k)
    for k in range(depth):
        s = lax.rem(zc + depth - k, depth) * 2 + (1 - xc)
        wait_rows(s)
        project(s, depth + k)

    for k in range(1, quarters):
        f = lax.rem(m + k, quarters)
        send(gain, gain_all.at[f], gsend.at[0], grecv.at[f], at_mp(f)).wait_recv()
    source = d // 2
    for s in range(groups):

        @pl.when(jnp.logical_not(jnp.logical_and(source == m, d == s)))
        def _(s=s):
            send(
                resid.at[:, :, pl.ds(0, block)],
                res_all.at[:, grp(s), :],
                rsend.at[0],
                rrecv.at[s],
                at_dp(partner),
            ).wait_recv()

    for k in range(1, quarters):
        f = lax.rem(m + k, quarters)
        for s in range(groups):
            slot = proj_in.at[f, :, grp(s), :]
            send(slot, slot, psend.at[0, 0], precv.at[f, s], at_mp(f)).wait_recv()

    proj = proj_out[m].astype(F32)
    for k in range(1, quarters):
        proj = proj + proj_in[lax.rem(m + k, quarters)].astype(F32)
    hidden = res_all[...].astype(F32) + proj
    gain_row = gain_all[source, pl.ds(lax.rem(d, 2) * quarters + m, 1), :]
    normed = hidden * gain_row
    rough = normed.astype(BF)
    squares = normed * normed
    ones = jnp.ones((8, block), F32)
    high = lax.Precision.HIGHEST
    sq_row = jnp.concatenate(
        [matmul(ones, squares[0], 1, 1, high), matmul(ones, squares[1], 1, 1, high)], axis=1
    )
    sq[me] = sq_row[:1]
    dots = matmul(rough[0], rough[1], 1, 1)
    dots_out[...] = dots.astype(BF).reshape(total, own_rows, pairs)
    dots_in[me] = dots_out[me]

    def exchange(which, make):
        def go(k, c):
            make(others(k), me, which, k).start()
            return c

        lax.fori_loop(1, total, go, 0)

    def settle(which, make):
        def go(k, c):
            make(others(k), others(k), which, k).wait_recv()
            return c

        lax.fori_loop(1, total, go, 0)

    def unsend(which, make):
        def go(k, c):
            make(others(k), me, which, k).wait_send()
            return c

        lax.fori_loop(1, total, go, 0)

    def along_all(src, dst):
        def make(t, slot, which, k):
            return send(
                src(t), dst.at[slot], allsend.at[which, k], allrecv.at[which, slot], at_any(t)
            )

        return make

    sq_make = along_all(lambda t: sq.at[me], sq)
    dot_make = along_all(lambda t: dots_out.at[t], dots_in)
    exchange(0, sq_make)
    exchange(1, dot_make)

    mine = pl.ds(pl.multiple_of(m * own_rows, own_rows), own_rows)
    ids = owner[mine, :] * here + local[mine, :]
    column = lax.broadcasted_iota(jnp.int32, (own_rows, pairs), 1)
    row = lax.broadcasted_iota(jnp.int32, (own_rows, pairs), 0) + me * own_rows
    own = (row == column).astype(F32)
    count = jnp.zeros((own_rows, pairs), F32)
    for k in range(ids.shape[1]):
        count = count + (ids[:, k : k + 1] == column).astype(F32)

    settle(0, sq_make)
    recip = lax.rsqrt(jnp.sum(sq[...], axis=0) + EPS)
    scale[...] = jnp.broadcast_to(recip, (block, 2 * pairs)).T
    settle(1, dot_make)
    recip_q = scale[pl.ds(pl.multiple_of(me * own_rows, own_rows), own_rows), :][:, :1]
    cosine = jnp.sum(dots_in[...].astype(F32), axis=0) * recip_q * recip[:, pairs:]
    expo = jnp.exp(cosine / TAU)
    prob = expo / jnp.sum((own + count) * expo, axis=1, keepdims=True)
    wts_neg = LOSS_SCALE * (count * prob) / TAU
    wts_pos = LOSS_SCALE * (own * (prob - 1.0)) / TAU
    along = (wts_neg + wts_pos) * cosine
    along_q = own * jnp.sum(along, axis=1, keepdims=True)
    extra_in[me] = jnp.concatenate(
        [
            jnp.sum(wts_pos, axis=0, keepdims=True),
            jnp.sum(along_q, axis=0, keepdims=True),
            jnp.sum(along, axis=0, keepdims=True),
        ],
        axis=1,
    )
    wts_in[me] = wts_neg.astype(BF)
    wts_make = along_all(lambda t: wts_in.at[me], wts_in)
    extra_make = along_all(lambda t: extra_in.at[me], extra_in)
    exchange(2, wts_make)
    exchange(3, extra_make)
    scaled = scale[...].reshape(2, pairs, block)
    unit = normed * scaled
    emb = unit.astype(BF)
    settle(3, extra_make)
    extra = jnp.sum(extra_in[...], axis=0)
    extra = jnp.broadcast_to(extra, (block, 3 * pairs)).T
    settle(2, wts_make)
    wts = wts_in[...].reshape(pairs, pairs)
    pos = extra[:pairs]
    grad_q = matmul(wts, emb[1], 1, 0) + pos * emb[1].astype(F32)
    dn_q = scaled[0] * (grad_q - unit[0] * extra[pairs : 2 * pairs])
    dh[m, 0] = (dn_q * gain_row).astype(BF)

    def send_dh(half):
        for k in range(1, quarters):
            t = lax.rem(m + k, quarters)
            slot = dh.at[m, half]
            c = send(slot, slot, hsend.at[half, k - 1], hrecv.at[half, m], at_mp(t))
            c.start()
            pending.append(c)

    send_dh(0)
    grad_e = matmul(wts, emb[0], 0, 0) + pos * emb[0].astype(F32)
    dn_e = scaled[1] * (grad_e - unit[1] * extra[2 * pairs :])
    dh[m, 1] = (dn_e * gain_row).astype(BF)
    send_dh(1)
    gg[me] = jnp.sum(dn_q * hidden[0] + dn_e * hidden[1], axis=0, keepdims=True)
    gg_make = along_all(lambda t: gg.at[me], gg)
    exchange(4, gg_make)
    for half in range(2):
        for k in range(1, quarters):
            f = lax.rem(m + k, quarters)
            slot = dh.at[f, half]
            send(slot, slot, hsend.at[0, 0], hrecv.at[half, f], at_mp(f)).wait_recv()

    def partial(s):
        value = jnp.zeros((2 * here, w_out.shape[1]), F32)
        for j in range(quarters):
            rows = dh[j, :, grp(s), :].reshape(2 * here, block)
            value = value + matmul(rows, w_out[j * block : (j + 1) * block, :], 1, 0)
        return value.reshape(2, here, -1)

    for k in range(depth):
        tz = lax.rem(zc + 1 + k, depth)
        xpart[k] = partial(tz * 2 + (1 - xc)).astype(BF)
        c = send(xpart.at[k], xin.at[k], xsend2.at[k], xrecv2.at[k], at_dp(partner))
        c.start()
        pending.append(c)
    last = None
    for k in range(depth):
        tz = lax.rem(zc + 1 + k, depth)
        value = partial(tz * 2 + xc)
        send(xpart.at[k], xin.at[k], xsend2.at[k], xrecv2.at[k], at_dp(partner)).wait_recv()
        value = value + xin[k].astype(F32)
        if k < depth - 1:
            zpart[k] = value.astype(BF)
            c = send(zpart.at[k], zin.at[k], zsend2.at[k], zrecv2.at[k], at_dp(tz * 2 + xc))
            c.start()
            pending.append(c)
        else:
            last = value
    attn_now = last
    for j in range(quarters):
        out = matmul(dh[j, 0], rows_a[0], 0, 0) + matmul(dh[j, 1], rows_a[1], 0, 0)
        weight_grad[j * block : (j + 1) * block, :] = out
    settle(4, gg_make)
    per = 2 * quarters
    gain_grad[...] = gg[pl.ds(m * per, per)]
    for k in range(depth - 1):
        send(zpart.at[k], zin.at[k], zsend2.at[k], zrecv2.at[k], at_dp(partner)).wait_recv()
        attn_now = attn_now + zin[k].astype(F32)
    attn_grad[...] = attn_now.astype(BF)

    for c in pending:
        c.wait_send()
    for is_self, c in res_sends:

        @pl.when(jnp.logical_not(is_self))
        def _(c=c):
            c.wait_send()

    for which, make in enumerate((sq_make, dot_make, wts_make, extra_make, gg_make)):
        unsend(which, make)


def by_feature(attn, resid, w_out, gain, neg_owner, neg_local):
    groups, quarters = lax.axis_size("dp"), lax.axis_size("mp")
    total = groups * quarters
    here = attn.shape[1]
    pairs = groups * here
    heads = attn.shape[2]
    block = w_out.shape[0] // quarters
    own_rows = pairs // total
    per = resid.shape[2] // block
    depth = groups // 2
    dma = pltpu.SemaphoreType.DMA
    vmem = pl.BlockSpec(memory_space=pltpu.VMEM)
    attn_grad, weight_grad, gain_grad = pl.pallas_call(
        functools.partial(fused, groups, quarters),
        out_shape=(
            jax.ShapeDtypeStruct(attn.shape, BF),
            jax.ShapeDtypeStruct(w_out.shape, F32),
            jax.ShapeDtypeStruct((per, 1, block), F32),
        ),
        in_specs=[vmem] * 6,
        out_specs=(vmem,) * 3,
        scratch_shapes=[
            pltpu.VMEM((2, pairs, heads), BF),
            pltpu.VMEM((2, pairs, block), BF),
            pltpu.VMEM((quarters, per, block), F32),
            pltpu.VMEM((quarters, 2, pairs, block), BF),
            pltpu.VMEM((quarters, 2, pairs, block), BF),
            pltpu.VMEM((total, 1, 2 * pairs), F32),
            pltpu.VMEM((total, own_rows, pairs), BF),
            pltpu.VMEM((total, own_rows, pairs), BF),
            pltpu.VMEM((total, own_rows, pairs), BF),
            pltpu.VMEM((total, 1, 3 * pairs), F32),
            pltpu.VMEM((2 * pairs, block), F32),
            pltpu.VMEM((total, 1, block), F32),
            pltpu.VMEM((quarters, 2, pairs, block), BF),
            pltpu.VMEM((depth, 2, here, heads), BF),
            pltpu.VMEM((depth, 2, here, heads), BF),
            pltpu.VMEM((depth - 1, 2, here, heads), BF),
            pltpu.VMEM((depth - 1, 2, here, heads), BF),
            dma((depth - 1,)),
            dma((depth,)),
            dma((groups,)),
            dma((per,)),
            dma((groups,)),
            dma((quarters - 1,)),
            dma((quarters,)),
            dma((quarters - 1, groups)),
            dma((quarters, groups)),
            dma((5, total)),
            dma((5, total)),
            dma((2, quarters - 1)),
            dma((2, quarters)),
            dma((depth,)),
            dma((depth,)),
            dma((depth - 1,)),
            dma((depth - 1,)),
        ],
        compiler_params=pltpu.CompilerParams(
            collective_id=0, has_side_effects=True, vmem_limit_bytes=48 * 1024 * 1024
        ),
    )(attn, resid, w_out, gain.reshape(per, block), neg_owner, neg_local)
    return attn_grad, weight_grad, gain_grad.reshape(-1)


def shards(attn, resid, w_out, gain, neg_owner, neg_local):
    groups, quarters = lax.axis_size("dp"), lax.axis_size("mp")
    here = attn.shape[1]
    block = w_out.shape[0] // quarters
    fits = block % 128 == 0 and resid.shape[2] == 2 * quarters * block and groups % 2 == 0
    fits = fits and groups * here <= 1024 and here % (16 * quarters) == 0
    plan = by_feature if fits else by_query
    return plan(attn, resid, w_out, gain, neg_owner, neg_local)


def solution(mesh):
    in_specs = (
        P(None, "dp", "mp"),
        P(None, "dp", "mp"),
        P("dp", "mp"),
        P("mp"),
        P("dp", None),
        P("dp", None),
    )
    out_specs = (P(None, "dp", "mp"), P("dp", "mp"), P("mp"))
    return jax.shard_map(shards, mesh=mesh, in_specs=in_specs, out_specs=out_specs, check_vma=False)
```

```python
import functools

import jax
import jax.numpy as jnp
from jax import lax
from jax.experimental import pallas as pl
from jax.experimental.pallas import tpu as pltpu
from jax.sharding import PartitionSpec as P

TAU = 0.05
LOSS_SCALE = 32.0
EPS = 1e-06


def by_query(attn, resid, w_out, gain, neg_owner, neg_local):
    groups = lax.axis_size("dp")
    pairs_here = attn.shape[1]
    feats = resid.shape[2]
    neg_count = neg_owner.shape[1]
    capacity = 2 * pairs_here * neg_count // groups
    rows_a = attn.reshape(2 * pairs_here, attn.shape[2])
    weight_full = lax.all_gather(w_out, "dp", axis=0, tiled=True)
    proj_part = lax.dot_general(
        rows_a, weight_full, (((1,), (1,)), ((), ())), preferred_element_type=jnp.float32
    )
    proj = lax.psum_scatter(proj_part, "mp", scatter_dimension=1, tiled=True)
    hidden = resid.reshape(2 * pairs_here, feats).astype(jnp.float32) + proj
    normed = hidden * gain
    squares = lax.psum(jnp.sum(normed * normed, axis=1), "mp")
    recip = lax.rsqrt(squares + EPS)[:, None]
    emb = (normed * recip).astype(jnp.bfloat16)
    query = emb[:pairs_here]
    docs = emb[pairs_here:]
    flat_owner = neg_owner.reshape(-1)
    flat_local = neg_local.reshape(-1)
    onehot = (flat_owner[:, None] == jnp.arange(groups, dtype=jnp.int32)[None, :]).astype(jnp.int32)
    ranks = jnp.sum((jnp.cumsum(onehot, axis=0) - 1) * onehot, axis=1)
    slot = flat_owner * capacity + ranks
    request = jnp.full((groups * capacity,), -1, jnp.int32).at[slot].set(flat_local)
    asked = lax.all_to_all(
        request.reshape(groups, capacity), "dp", split_axis=0, concat_axis=0, tiled=True
    )
    valid = asked >= 0
    safe_rows = jnp.maximum(asked, 0)
    outgoing = jnp.where(valid[:, :, None], docs[safe_rows], jnp.zeros((), jnp.bfloat16))
    fetched = lax.all_to_all(outgoing, "dp", split_axis=0, concat_axis=0, tiled=True)
    neg_emb = fetched.reshape(groups * capacity, feats)[slot].reshape(pairs_here, neg_count, feats)
    pos_part = jnp.sum(query.astype(jnp.float32) * docs.astype(jnp.float32), axis=1)
    neg_part = jnp.einsum("pd,pkd->pk", query, neg_emb, preferred_element_type=jnp.float32)
    partial_value = jnp.concatenate([pos_part[:, None], neg_part], axis=1)
    scores = lax.psum(partial_value, "mp") / TAU
    expo = jnp.exp(scores)
    prob = expo / jnp.sum(expo, axis=1, keepdims=True)
    first = (jnp.arange(neg_count + 1) == 0).astype(jnp.float32)[None, :]
    wts = LOSS_SCALE * (prob - first) / TAU
    query_f = query.astype(jnp.float32)
    grad_query = wts[:, 0:1] * docs.astype(jnp.float32) + jnp.einsum(
        "pk,pkd->pd", wts[:, 1:], neg_emb, preferred_element_type=jnp.float32
    )
    terms = (wts[:, 1:, None] * query_f[:, None, :]).astype(jnp.bfloat16)
    slot_buffer = (
        jnp.zeros((groups * capacity, feats), jnp.bfloat16).at[slot].set(terms.reshape(-1, feats))
    )
    returned = lax.all_to_all(
        slot_buffer.reshape(groups, capacity, feats), "dp", split_axis=0, concat_axis=0, tiled=True
    )
    targets = jnp.where(valid, asked, pairs_here).reshape(-1)
    selector = (jnp.arange(pairs_here, dtype=jnp.int32)[:, None] == targets[None, :]).astype(
        jnp.bfloat16
    )
    grad_docs = wts[:, 0:1] * query_f + jnp.dot(
        selector, returned.reshape(-1, feats), preferred_element_type=jnp.float32
    )
    demb = jnp.concatenate([grad_query, grad_docs], axis=0)
    inner = lax.psum(jnp.sum(normed * demb, axis=1), "mp")[:, None]
    dnorm = recip * demb - recip * recip * recip * normed * inner
    gain_grad = lax.psum(jnp.sum(dnorm * hidden, axis=0), "dp")
    dh = (dnorm * gain).astype(jnp.bfloat16)
    dh_full = lax.all_gather(dh, "mp", axis=1, tiled=True)
    attn_grad = (
        jnp.dot(dh_full, weight_full, preferred_element_type=jnp.float32)
        .astype(jnp.bfloat16)
        .reshape(attn.shape)
    )
    weight_grad = lax.psum_scatter(
        lax.dot_general(
            dh_full, rows_a, (((0,), (0,)), ((), ())), preferred_element_type=jnp.float32
        ),
        "dp",
        scatter_dimension=0,
        tiled=True,
    )
    return (attn_grad, weight_grad, gain_grad)


MESH = pl.DeviceIdType.MESH
BF = jnp.bfloat16
F32 = jnp.float32


def matmul(left, right, left_dim, right_dim, precision=None):
    return lax.dot_general(
        left,
        right,
        (((left_dim,), (right_dim,)), ((), ())),
        precision=precision,
        preferred_element_type=F32,
    )


def fused(
    groups,
    quarters,
    attn,
    resid,
    w_hbm,
    gain,
    owner_hbm,
    local_hbm,
    attn_grad,
    weight_grad,
    gain_grad,
    w_out,
    owner,
    local,
    rows_a,
    res_all,
    gain_all,
    proj_out,
    proj_in,
    sq_in,
    sq_all,
    dots_out,
    dots_in,
    half_out,
    half_in,
    wts_all,
    extra_in,
    extra_all,
    scale,
    gg,
    dh,
    xpart,
    xin,
    zpart,
    zin,
    load,
    zsend,
    xsend,
    arecv,
    rsend,
    rrecv,
    gsend,
    grecv,
    psend,
    precv,
    msend,
    mrecv,
    dsend,
    drecv,
    hsend,
    hrecv,
    xsend2,
    xrecv2,
    zsend2,
    zrecv2,
):
    d, m = lax.axis_index("dp"), lax.axis_index("mp")
    total = groups * quarters
    me = d * quarters + m
    here = attn.shape[1]
    pairs = groups * here
    block = w_out.shape[0] // quarters
    pair, across = m + 1 - 2 * lax.rem(m, 2), lax.rem(m + 2, quarters)
    own_rows = pairs // total
    zc, xc = d // 2, d % 2
    depth = groups // 2
    partner = zc * 2 + (1 - xc)

    def at_dp(t):
        return (t, m)

    def at_mp(t):
        return (d, t)

    def at_any(t):
        return (t // quarters, t % quarters)

    def send(src, dst, s, r, dev):
        return pltpu.make_async_remote_copy(
            src_ref=src, dst_ref=dst, send_sem=s, recv_sem=r, device_id=dev, device_id_type=MESH
        )

    def grp(s):
        return pl.ds(pl.multiple_of(s * here, here), here)

    def others(k):
        return lax.rem(me + k, total)

    barrier = pltpu.get_barrier_semaphore()

    loads = [
        pltpu.make_async_copy(attn, rows_a.at[:, grp(d), :], load.at[0]),
        pltpu.make_async_copy(w_hbm, w_out, load.at[1]),
        pltpu.make_async_copy(gain, gain_all.at[m], load.at[2]),
        pltpu.make_async_copy(owner_hbm, owner, load.at[3]),
        pltpu.make_async_copy(local_hbm, local, load.at[4]),
    ]
    for c in loads:
        c.start()

    def greet(k, c):
        pl.semaphore_signal(barrier, inc=1, device_id=at_any(others(k)), device_id_type=MESH)
        return c

    lax.fori_loop(1, total, greet, 0)
    pl.semaphore_wait(barrier, total - 1)

    pending = []
    first = send(attn, rows_a.at[:, grp(d), :], xsend.at[0], arecv.at[d], at_dp(partner))
    first.start()
    pending.append(first)
    for k in range(1, depth):
        t = lax.rem(zc + k, depth) * 2 + xc
        c = send(attn, rows_a.at[:, grp(d), :], zsend.at[k - 1], arecv.at[d], at_dp(t))
        c.start()
        pending.append(c)
    for k in range(1, quarters):
        c = send(gain, gain_all.at[m], gsend.at[k - 1], grecv.at[m], at_mp(lax.rem(m + k, quarters)))
        c.start()
        pending.append(c)

    res_sends = []
    for a in range(2):
        for j in range(quarters):
            cols = pl.ds((a * quarters + j) * block, block)
            td = 2 * m + a
            is_self = jnp.logical_and(td == d, m == j)
            c = send(
                resid.at[:, :, cols],
                res_all.at[:, grp(d), :],
                rsend.at[a * quarters + j],
                rrecv.at[d],
                (td, jnp.int32(j)),
            )
            res_sends.append((is_self, c))

            @pl.when(jnp.logical_not(is_self))
            def _(c=c):
                c.start()

            @pl.when(is_self)
            def _(cols=cols):
                c = pltpu.make_async_copy(
                    resid.at[:, :, cols], res_all.at[:, grp(d), :], load.at[5]
                )
                c.start()
                c.wait()

    def project(s, i):
        part = matmul(rows_a[:, grp(s), :].reshape(2 * here, -1), w_out[...], 1, 1)
        for j in range(quarters):
            piece = part[:, j * block : (j + 1) * block].astype(BF)
            proj_out[j, :, grp(s), :] = piece.reshape(2, here, block)
        for k in range(1, quarters):
            t = lax.rem(m + k, quarters)
            c = send(
                proj_out.at[t, :, grp(s), :],
                proj_in.at[m, :, grp(s), :],
                psend.at[k - 1, i],
                precv.at[m, s],
                at_mp(t),
            )
            c.start()
            pending.append(c)

    def wait_rows(s):
        send(attn, rows_a.at[:, grp(s), :], zsend.at[0], arecv.at[s], at_dp(partner)).wait_recv()

    loads[0].wait()
    loads[1].wait()
    project(d, 0)
    for k in range(1, depth):
        s = lax.rem(zc + depth - k, depth) * 2 + xc
        wait_rows(s)
        slot = rows_a.at[:, grp(s), :]
        c = send(slot, slot, xsend.at[k], arecv.at[s], at_dp(partner))
        c.start()
        pending.append(c)
        project(s, k)
    for k in range(depth):
        s = lax.rem(zc + depth - k, depth) * 2 + (1 - xc)
        wait_rows(s)
        project(s, depth + k)

    for c in loads[2:]:
        c.wait()
    for k in range(1, quarters):
        f = lax.rem(m + k, quarters)
        send(gain, gain_all.at[f], gsend.at[0], grecv.at[f], at_mp(f)).wait_recv()
    source = d // 2
    for s in range(groups):

        @pl.when(jnp.logical_not(jnp.logical_and(source == m, d == s)))
        def _(s=s):
            send(
                resid.at[:, :, pl.ds(0, block)],
                res_all.at[:, grp(s), :],
                rsend.at[0],
                rrecv.at[s],
                at_dp(partner),
            ).wait_recv()

    for k in range(1, quarters):
        f = lax.rem(m + k, quarters)
        for s in range(groups):
            slot = proj_in.at[f, :, grp(s), :]
            send(slot, slot, psend.at[0, 0], precv.at[f, s], at_mp(f)).wait_recv()

    proj = proj_out[m].astype(F32)
    for k in range(1, quarters):
        proj = proj + proj_in[lax.rem(m + k, quarters)].astype(F32)
    hidden = res_all[...].astype(F32) + proj
    gain_row = gain_all[source, pl.ds(lax.rem(d, 2) * quarters + m, 1), :]
    normed = hidden * gain_row
    rough = normed.astype(BF)
    squares = normed * normed
    ones = jnp.ones((8, block), F32)
    high = lax.Precision.HIGHEST
    sq_row = jnp.concatenate(
        [matmul(ones, squares[0], 1, 1, high), matmul(ones, squares[1], 1, 1, high)], axis=1
    )
    dots = matmul(rough[0], rough[1], 1, 1).astype(BF)
    dots = dots.reshape(groups, quarters, own_rows, pairs)
    for j in range(quarters):
        dots_out[j] = dots[:, j]

    def to_mp(which, src, dst):
        for k in range(1, quarters):
            t = lax.rem(m + k, quarters)
            c = send(src(t), dst.at[m], msend.at[which, k - 1], mrecv.at[which, m], at_mp(t))
            c.start()
            pending.append(c)

    def from_mp(which, dst):
        for k in range(1, quarters):
            f = lax.rem(m + k, quarters)
            slot = dst.at[f]
            send(slot, slot, msend.at[which, 0], mrecv.at[which, f], at_mp(f)).wait_recv()

    def to_dp(which, src, dst):
        for k in range(1, groups):
            t = lax.rem(d + k, groups)
            c = send(src(t), dst.at[d], dsend.at[which, k - 1], drecv.at[which, d], at_dp(t))
            c.start()
            pending.append(c)

    def from_dp(which, dst):
        for k in range(1, groups):
            f = lax.rem(d + k, groups)
            slot = dst.at[f]
            send(slot, slot, dsend.at[which, 0], drecv.at[which, f], at_dp(f)).wait_recv()

    to_mp(0, lambda t: dots_out.at[t], dots_in)
    sq_in[m] = sq_row[:1]
    to_mp(1, lambda t: sq_in.at[m], sq_in)

    mine = pl.ds(pl.multiple_of(m * own_rows, own_rows), own_rows)
    ids = owner[mine, :] * here + local[mine, :]
    column = lax.broadcasted_iota(jnp.int32, (own_rows, pairs), 1)
    row = lax.broadcasted_iota(jnp.int32, (own_rows, pairs), 0) + me * own_rows
    own = (row == column).astype(F32)
    count = jnp.zeros((own_rows, pairs), F32)
    for k in range(ids.shape[1]):
        count = count + (ids[:, k : k + 1] == column).astype(F32)

    from_mp(1, sq_in)
    sq_all[d] = jnp.sum(sq_in[...], axis=0)
    to_dp(0, lambda t: sq_all.at[d], sq_all)
    from_mp(0, dots_in)
    partial_dots = dots_out[m].astype(F32)
    for k in range(1, quarters):
        partial_dots = partial_dots + dots_in[lax.rem(m + k, quarters)].astype(F32)
    half_out[...] = partial_dots.astype(BF)
    to_dp(1, lambda t: half_out.at[t], half_in)
    from_dp(0, sq_all)
    recip = lax.rsqrt(jnp.sum(sq_all[...], axis=0) + EPS)
    scale[...] = jnp.broadcast_to(recip, (block, 2 * pairs)).T
    half_in[d] = half_out[d]
    from_dp(1, half_in)
    recip_q = scale[pl.ds(pl.multiple_of(me * own_rows, own_rows), own_rows), :][:, :1]
    cosine = jnp.sum(half_in[...].astype(F32), axis=0) * recip_q * recip[:, pairs:]
    expo = jnp.exp(cosine / TAU)
    prob = expo / jnp.sum((own + count) * expo, axis=1, keepdims=True)
    wts_neg = LOSS_SCALE * (count * prob) / TAU
    wts_pos = LOSS_SCALE * (own * (prob - 1.0)) / TAU
    along = (wts_neg + wts_pos) * cosine
    along_q = own * jnp.sum(along, axis=1, keepdims=True)
    extra_in[d] = jnp.concatenate(
        [
            jnp.sum(wts_pos, axis=0, keepdims=True),
            jnp.sum(along_q, axis=0, keepdims=True),
            jnp.sum(along, axis=0, keepdims=True),
        ],
        axis=1,
    )
    wts_all[m, d] = wts_neg.astype(BF)
    to_dp(2, lambda t: wts_all.at[m, d], wts_all.at[m])
    to_dp(3, lambda t: extra_in.at[d], extra_in)
    scaled = scale[...].reshape(2, pairs, block)
    unit = normed * scaled
    emb = unit.astype(BF)
    from_dp(2, wts_all.at[m])
    to_mp(2, lambda t: wts_all.at[m], wts_all)
    from_dp(3, extra_in)
    extra_all[m] = jnp.sum(extra_in[...], axis=0)
    to_mp(3, lambda t: extra_all.at[m], extra_all)
    from_mp(3, extra_all)
    extra = jnp.sum(extra_all[...], axis=0)
    extra = jnp.broadcast_to(extra, (block, 3 * pairs)).T
    from_mp(2, wts_all)
    wts = jnp.stack([wts_all[j] for j in range(quarters)], axis=1).reshape(pairs, pairs)
    pos = extra[:pairs]
    grad_q = matmul(wts, emb[1], 1, 0) + pos * emb[1].astype(F32)
    dn_q = scaled[0] * (grad_q - unit[0] * extra[pairs : 2 * pairs])
    here_cols = pl.ds(pl.multiple_of(m * block, block), block)
    dh[0, :, here_cols] = (dn_q * gain_row).astype(BF)

    def dh_slot(half, t):
        return dh.at[half, :, pl.ds(pl.multiple_of(t * block, block), block)]

    def send_dh(half, t, k, dev):
        slot = dh_slot(half, t)
        c = send(slot, slot, hsend.at[half, k], hrecv.at[half, t], at_mp(dev))
        c.start()
        pending.append(c)

    def wait_dh(half, t):
        slot = dh_slot(half, t)
        send(slot, slot, hsend.at[0, 0], hrecv.at[half, t], at_mp(pair)).wait_recv()

    send_dh(0, m, 0, across)
    send_dh(0, m, 1, pair)
    grad_e = matmul(wts, emb[0], 0, 0) + pos * emb[0].astype(F32)
    dn_e = scaled[1] * (grad_e - unit[1] * extra[2 * pairs :])
    dh[1, :, here_cols] = (dn_e * gain_row).astype(BF)
    send_dh(1, m, 0, across)
    send_dh(1, m, 1, pair)
    gg[m, d] = jnp.sum(dn_q * hidden[0] + dn_e * hidden[1], axis=0, keepdims=True)
    to_dp(4, lambda t: gg.at[m, d], gg.at[m])
    for half in range(2):
        wait_dh(half, across)
        send_dh(half, across, 2, pair)
    from_dp(4, gg.at[m])
    to_mp(4, lambda t: gg.at[m], gg)
    for half in range(2):
        wait_dh(half, pair)
        wait_dh(half, pair + across - m)

    def partial(s):
        rows = dh[:, grp(s), :].reshape(2 * here, -1)
        return matmul(rows, w_out[...], 1, 0).reshape(2, here, -1)

    for k in range(depth):
        tz = lax.rem(zc + 1 + k, depth)
        xpart[k] = partial(tz * 2 + (1 - xc)).astype(BF)
        c = send(xpart.at[k], xin.at[k], xsend2.at[k], xrecv2.at[k], at_dp(partner))
        c.start()
        pending.append(c)
    last = None
    for k in range(depth):
        tz = lax.rem(zc + 1 + k, depth)
        value = partial(tz * 2 + xc)
        send(xpart.at[k], xin.at[k], xsend2.at[k], xrecv2.at[k], at_dp(partner)).wait_recv()
        value = value + xin[k].astype(F32)
        if k < depth - 1:
            zpart[k] = value.astype(BF)
            c = send(zpart.at[k], zin.at[k], zsend2.at[k], zrecv2.at[k], at_dp(tz * 2 + xc))
            c.start()
            pending.append(c)
        else:
            last = value
    attn_now = last
    for j in range(quarters):
        cols = pl.ds(j * block, block)
        out = matmul(dh[0, :, cols], rows_a[0], 0, 0) + matmul(dh[1, :, cols], rows_a[1], 0, 0)
        weight_grad[j * block : (j + 1) * block, :] = out
    from_mp(4, gg)
    for a in range(2):
        for j in range(quarters):
            gain_grad[a * quarters + j] = gg[j, 2 * m + a]
    for k in range(depth - 1):
        send(zpart.at[k], zin.at[k], zsend2.at[k], zrecv2.at[k], at_dp(partner)).wait_recv()
        attn_now = attn_now + zin[k].astype(F32)
    attn_grad[...] = attn_now.astype(BF)

    for c in pending:
        c.wait_send()
    for is_self, c in res_sends:

        @pl.when(jnp.logical_not(is_self))
        def _(c=c):
            c.wait_send()


def by_feature(attn, resid, w_out, gain, neg_owner, neg_local):
    groups, quarters = lax.axis_size("dp"), lax.axis_size("mp")
    total = groups * quarters
    here = attn.shape[1]
    pairs = groups * here
    heads = attn.shape[2]
    block = w_out.shape[0] // quarters
    own_rows = pairs // total
    per = resid.shape[2] // block
    depth = groups // 2
    dma = pltpu.SemaphoreType.DMA
    vmem = pl.BlockSpec(memory_space=pltpu.VMEM)
    attn_grad, weight_grad, gain_grad = pl.pallas_call(
        functools.partial(fused, groups, quarters),
        out_shape=(
            jax.ShapeDtypeStruct(attn.shape, BF),
            jax.ShapeDtypeStruct(w_out.shape, F32),
            jax.ShapeDtypeStruct((per, 1, block), F32),
        ),
        in_specs=[pl.BlockSpec(memory_space=pltpu.HBM)] * 6,
        out_specs=(vmem,) * 3,
        scratch_shapes=[
            pltpu.VMEM(w_out.shape, BF),
            pltpu.VMEM(neg_owner.shape, jnp.int32),
            pltpu.VMEM(neg_local.shape, jnp.int32),
            pltpu.VMEM((2, pairs, heads), BF),
            pltpu.VMEM((2, pairs, block), BF),
            pltpu.VMEM((quarters, per, block), F32),
            pltpu.VMEM((quarters, 2, pairs, block), BF),
            pltpu.VMEM((quarters, 2, pairs, block), BF),
            pltpu.VMEM((quarters, 1, 2 * pairs), F32),
            pltpu.VMEM((groups, 1, 2 * pairs), F32),
            pltpu.VMEM((quarters, groups, own_rows, pairs), BF),
            pltpu.VMEM((quarters, groups, own_rows, pairs), BF),
            pltpu.VMEM((groups, own_rows, pairs), BF),
            pltpu.VMEM((groups, own_rows, pairs), BF),
            pltpu.VMEM((quarters, groups, own_rows, pairs), BF),
            pltpu.VMEM((groups, 1, 3 * pairs), F32),
            pltpu.VMEM((quarters, 1, 3 * pairs), F32),
            pltpu.VMEM((2 * pairs, block), F32),
            pltpu.VMEM((quarters, groups, 1, block), F32),
            pltpu.VMEM((2, pairs, quarters * block), BF),
            pltpu.VMEM((depth, 2, here, heads), BF),
            pltpu.VMEM((depth, 2, here, heads), BF),
            pltpu.VMEM((depth - 1, 2, here, heads), BF),
            pltpu.VMEM((depth - 1, 2, here, heads), BF),
            dma((6,)),
            dma((depth - 1,)),
            dma((depth,)),
            dma((groups,)),
            dma((per,)),
            dma((groups,)),
            dma((quarters - 1,)),
            dma((quarters,)),
            dma((quarters - 1, groups)),
            dma((quarters, groups)),
            dma((5, quarters - 1)),
            dma((5, quarters)),
            dma((5, groups - 1)),
            dma((5, groups)),
            dma((2, 3)),
            dma((2, quarters)),
            dma((depth,)),
            dma((depth,)),
            dma((depth - 1,)),
            dma((depth - 1,)),
        ],
        compiler_params=pltpu.CompilerParams(
            collective_id=0, has_side_effects=True, vmem_limit_bytes=48 * 1024 * 1024
        ),
    )(attn, resid, w_out, gain.reshape(per, block), neg_owner, neg_local)
    return attn_grad, weight_grad, gain_grad.reshape(-1)


def shards(attn, resid, w_out, gain, neg_owner, neg_local):
    groups, quarters = lax.axis_size("dp"), lax.axis_size("mp")
    here = attn.shape[1]
    block = w_out.shape[0] // quarters
    fits = quarters == 4 and block % 128 == 0 and resid.shape[2] == 2 * quarters * block and groups % 2 == 0
    fits = fits and groups * here <= 1024 and here % (16 * quarters) == 0
    plan = by_feature if fits else by_query
    return plan(attn, resid, w_out, gain, neg_owner, neg_local)


def solution(mesh):
    in_specs = (
        P(None, "dp", "mp"),
        P(None, "dp", "mp"),
        P("dp", "mp"),
        P("mp"),
        P("dp", None),
        P("dp", None),
    )
    out_specs = (P(None, "dp", "mp"), P("dp", "mp"), P("mp"))
    return jax.shard_map(shards, mesh=mesh, in_specs=in_specs, out_specs=out_specs, check_vma=False)
```

```python
import functools

import jax
import jax.numpy as jnp
from jax import lax
from jax.experimental import pallas as pl
from jax.experimental.pallas import tpu as pltpu
from jax.sharding import PartitionSpec as P

TAU = 0.05
LOSS_SCALE = 32.0
EPS = 1e-06


def by_query(attn, resid, w_out, gain, neg_owner, neg_local):
    groups = lax.axis_size("dp")
    pairs_here = attn.shape[1]
    feats = resid.shape[2]
    neg_count = neg_owner.shape[1]
    capacity = 2 * pairs_here * neg_count // groups
    rows_a = attn.reshape(2 * pairs_here, attn.shape[2])
    weight_full = lax.all_gather(w_out, "dp", axis=0, tiled=True)
    proj_part = lax.dot_general(
        rows_a, weight_full, (((1,), (1,)), ((), ())), preferred_element_type=jnp.float32
    )
    proj = lax.psum_scatter(proj_part, "mp", scatter_dimension=1, tiled=True)
    hidden = resid.reshape(2 * pairs_here, feats).astype(jnp.float32) + proj
    normed = hidden * gain
    squares = lax.psum(jnp.sum(normed * normed, axis=1), "mp")
    recip = lax.rsqrt(squares + EPS)[:, None]
    emb = (normed * recip).astype(jnp.bfloat16)
    query = emb[:pairs_here]
    docs = emb[pairs_here:]
    flat_owner = neg_owner.reshape(-1)
    flat_local = neg_local.reshape(-1)
    onehot = (flat_owner[:, None] == jnp.arange(groups, dtype=jnp.int32)[None, :]).astype(jnp.int32)
    ranks = jnp.sum((jnp.cumsum(onehot, axis=0) - 1) * onehot, axis=1)
    slot = flat_owner * capacity + ranks
    request = jnp.full((groups * capacity,), -1, jnp.int32).at[slot].set(flat_local)
    asked = lax.all_to_all(
        request.reshape(groups, capacity), "dp", split_axis=0, concat_axis=0, tiled=True
    )
    valid = asked >= 0
    safe_rows = jnp.maximum(asked, 0)
    outgoing = jnp.where(valid[:, :, None], docs[safe_rows], jnp.zeros((), jnp.bfloat16))
    fetched = lax.all_to_all(outgoing, "dp", split_axis=0, concat_axis=0, tiled=True)
    neg_emb = fetched.reshape(groups * capacity, feats)[slot].reshape(pairs_here, neg_count, feats)
    pos_part = jnp.sum(query.astype(jnp.float32) * docs.astype(jnp.float32), axis=1)
    neg_part = jnp.einsum("pd,pkd->pk", query, neg_emb, preferred_element_type=jnp.float32)
    partial_value = jnp.concatenate([pos_part[:, None], neg_part], axis=1)
    scores = lax.psum(partial_value, "mp") / TAU
    expo = jnp.exp(scores)
    prob = expo / jnp.sum(expo, axis=1, keepdims=True)
    first = (jnp.arange(neg_count + 1) == 0).astype(jnp.float32)[None, :]
    wts = LOSS_SCALE * (prob - first) / TAU
    query_f = query.astype(jnp.float32)
    grad_query = wts[:, 0:1] * docs.astype(jnp.float32) + jnp.einsum(
        "pk,pkd->pd", wts[:, 1:], neg_emb, preferred_element_type=jnp.float32
    )
    terms = (wts[:, 1:, None] * query_f[:, None, :]).astype(jnp.bfloat16)
    slot_buffer = (
        jnp.zeros((groups * capacity, feats), jnp.bfloat16).at[slot].set(terms.reshape(-1, feats))
    )
    returned = lax.all_to_all(
        slot_buffer.reshape(groups, capacity, feats), "dp", split_axis=0, concat_axis=0, tiled=True
    )
    targets = jnp.where(valid, asked, pairs_here).reshape(-1)
    selector = (jnp.arange(pairs_here, dtype=jnp.int32)[:, None] == targets[None, :]).astype(
        jnp.bfloat16
    )
    grad_docs = wts[:, 0:1] * query_f + jnp.dot(
        selector, returned.reshape(-1, feats), preferred_element_type=jnp.float32
    )
    demb = jnp.concatenate([grad_query, grad_docs], axis=0)
    inner = lax.psum(jnp.sum(normed * demb, axis=1), "mp")[:, None]
    dnorm = recip * demb - recip * recip * recip * normed * inner
    gain_grad = lax.psum(jnp.sum(dnorm * hidden, axis=0), "dp")
    dh = (dnorm * gain).astype(jnp.bfloat16)
    dh_full = lax.all_gather(dh, "mp", axis=1, tiled=True)
    attn_grad = (
        jnp.dot(dh_full, weight_full, preferred_element_type=jnp.float32)
        .astype(jnp.bfloat16)
        .reshape(attn.shape)
    )
    weight_grad = lax.psum_scatter(
        lax.dot_general(
            dh_full, rows_a, (((0,), (0,)), ((), ())), preferred_element_type=jnp.float32
        ),
        "dp",
        scatter_dimension=0,
        tiled=True,
    )
    return (attn_grad, weight_grad, gain_grad)


MESH = pl.DeviceIdType.MESH
BF = jnp.bfloat16
F32 = jnp.float32


def matmul(left, right, left_dim, right_dim, precision=None):
    return lax.dot_general(
        left,
        right,
        (((left_dim,), (right_dim,)), ((), ())),
        precision=precision,
        preferred_element_type=F32,
    )


def fused(
    groups,
    quarters,
    attn,
    resid,
    w_hbm,
    gain,
    owner_hbm,
    local_hbm,
    attn_grad,
    weight_grad,
    gain_grad,
    w_out,
    owner,
    local,
    rows_a,
    res_all,
    gain_all,
    proj_out,
    proj_in,
    sq_in,
    sq_all,
    dots_out,
    dots_in,
    half_out,
    half_in,
    wts_all,
    extra_in,
    extra_all,
    scale,
    gg,
    dh,
    xpart,
    xin,
    zpart,
    zin,
    load,
    zsend,
    xsend,
    arecv,
    rsend,
    rrecv,
    gsend,
    grecv,
    psend,
    precv,
    msend,
    mrecv,
    dsend,
    drecv,
    hsend,
    hrecv,
    xsend2,
    xrecv2,
    zsend2,
    zrecv2,
):
    d, m = lax.axis_index("dp"), lax.axis_index("mp")
    total = groups * quarters
    me = d * quarters + m
    here = attn.shape[1]
    pairs = groups * here
    block = w_out.shape[0] // quarters
    pair, across = m + 1 - 2 * lax.rem(m, 2), lax.rem(m + 2, quarters)
    own_rows = pairs // total
    zc, xc = d // 2, d % 2
    depth = groups // 2
    partner = zc * 2 + (1 - xc)

    def at_dp(t):
        return (t, m)

    def at_mp(t):
        return (d, t)

    def at_any(t):
        return (t // quarters, t % quarters)

    def send(src, dst, s, r, dev):
        return pltpu.make_async_remote_copy(
            src_ref=src, dst_ref=dst, send_sem=s, recv_sem=r, device_id=dev, device_id_type=MESH
        )

    def grp(s):
        return pl.ds(pl.multiple_of(s * here, here), here)

    def others(k):
        return lax.rem(me + k, total)

    barrier = pltpu.get_barrier_semaphore()

    loads = [
        pltpu.make_async_copy(attn, rows_a.at[:, grp(d), :], load.at[0]),
        pltpu.make_async_copy(w_hbm, w_out, load.at[1]),
        pltpu.make_async_copy(gain, gain_all.at[m], load.at[2]),
        pltpu.make_async_copy(owner_hbm, owner, load.at[3]),
        pltpu.make_async_copy(local_hbm, local, load.at[4]),
    ]
    for c in loads:
        c.start()

    def greet(k, c):
        pl.semaphore_signal(barrier, inc=1, device_id=at_any(others(k)), device_id_type=MESH)
        return c

    lax.fori_loop(1, total, greet, 0)
    pl.semaphore_wait(barrier, total - 1)

    pending = []
    first = send(attn, rows_a.at[:, grp(d), :], xsend.at[0], arecv.at[d], at_dp(partner))
    first.start()
    pending.append(first)
    middle = (zc + 1) // 2 == 1
    near = zc + 1 - 2 * lax.rem(zc, 2)
    c = send(attn, rows_a.at[:, grp(d), :], zsend.at[0], arecv.at[d], at_dp(near * 2 + xc))
    c.start()
    pending.append(c)
    passed = [send(attn, rows_a.at[:, grp(d), :], zsend.at[1], arecv.at[d], at_dp((3 - zc) * 2 + xc))]

    @pl.when(middle)
    def _():
        passed[0].start()

    for k in range(1, quarters):
        c = send(gain, gain_all.at[m], gsend.at[k - 1], grecv.at[m], at_mp(lax.rem(m + k, quarters)))
        c.start()
        pending.append(c)

    res_sends = []
    for a in range(2):
        for j in range(quarters):
            cols = pl.ds((a * quarters + j) * block, block)
            td = 2 * m + a
            is_self = jnp.logical_and(td == d, m == j)
            c = send(
                resid.at[:, :, cols],
                res_all.at[:, grp(d), :],
                rsend.at[a * quarters + j],
                rrecv.at[d],
                (td, jnp.int32(j)),
            )
            res_sends.append((is_self, c))

            @pl.when(jnp.logical_not(is_self))
            def _(c=c):
                c.start()

            @pl.when(is_self)
            def _(cols=cols):
                c = pltpu.make_async_copy(
                    resid.at[:, :, cols], res_all.at[:, grp(d), :], load.at[5]
                )
                c.start()
                c.wait()

    def project(s, i):
        part = matmul(rows_a[:, grp(s), :].reshape(2 * here, -1), w_out[...], 1, 1)
        for j in range(quarters):
            piece = part[:, j * block : (j + 1) * block].astype(BF)
            proj_out[j, :, grp(s), :] = piece.reshape(2, here, block)
        for k in range(1, quarters):
            t = lax.rem(m + k, quarters)
            c = send(
                proj_out.at[t, :, grp(s), :],
                proj_in.at[m, :, grp(s), :],
                psend.at[k - 1, i],
                precv.at[m, s],
                at_mp(t),
            )
            c.start()
            pending.append(c)

    def wait_rows(s):
        send(attn, rows_a.at[:, grp(s), :], zsend.at[0], arecv.at[s], at_dp(partner)).wait_recv()

    loads[0].wait()
    loads[1].wait()
    project(d, 0)
    half = zc // 2
    nearest = (near, 2 - half, 3 - 3 * half)
    for k in range(1, depth):
        s = nearest[k - 1] * 2 + xc
        onward = 3 - zc if k == 1 else 3 * (zc - 1)
        wait_rows(s)
        slot = rows_a.at[:, grp(s), :]
        c = send(slot, slot, zsend.at[k + 1], arecv.at[s], at_dp(onward * 2 + xc))
        passed.append(c)

        @pl.when(middle)
        def _(c=c):
            c.start()

        c = send(slot, slot, xsend.at[k], arecv.at[s], at_dp(partner))
        c.start()
        pending.append(c)
        project(s, k)
    for k in range(depth):
        s = (zc if k == 0 else nearest[k - 1]) * 2 + (1 - xc)
        wait_rows(s)
        project(s, depth + k)

    for c in loads[2:]:
        c.wait()
    for k in range(1, quarters):
        f = lax.rem(m + k, quarters)
        send(gain, gain_all.at[f], gsend.at[0], grecv.at[f], at_mp(f)).wait_recv()
    source = d // 2
    for s in range(groups):

        @pl.when(jnp.logical_not(jnp.logical_and(source == m, d == s)))
        def _(s=s):
            send(
                resid.at[:, :, pl.ds(0, block)],
                res_all.at[:, grp(s), :],
                rsend.at[0],
                rrecv.at[s],
                at_dp(partner),
            ).wait_recv()

    for k in range(1, quarters):
        f = lax.rem(m + k, quarters)
        for s in range(groups):
            slot = proj_in.at[f, :, grp(s), :]
            send(slot, slot, psend.at[0, 0], precv.at[f, s], at_mp(f)).wait_recv()

    proj = proj_out[m].astype(F32)
    for k in range(1, quarters):
        proj = proj + proj_in[lax.rem(m + k, quarters)].astype(F32)
    hidden = res_all[...].astype(F32) + proj
    gain_row = gain_all[source, pl.ds(lax.rem(d, 2) * quarters + m, 1), :]
    normed = hidden * gain_row
    rough = normed.astype(BF)
    dots = matmul(rough[0], rough[1], 1, 1).astype(BF)
    dots = dots.reshape(groups, quarters, own_rows, pairs)
    for j in range(quarters):
        dots_out[j] = dots[:, j]

    def to_mp(which, src, dst):
        for k in range(1, quarters):
            t = lax.rem(m + k, quarters)
            c = send(src(t), dst.at[m], msend.at[which, k - 1], mrecv.at[which, m], at_mp(t))
            c.start()
            pending.append(c)

    def from_mp(which, dst):
        for k in range(1, quarters):
            f = lax.rem(m + k, quarters)
            slot = dst.at[f]
            send(slot, slot, msend.at[which, 0], mrecv.at[which, f], at_mp(f)).wait_recv()

    def to_dp(which, src, dst):
        for k in range(1, groups):
            t = lax.rem(d + k, groups)
            c = send(src(t), dst.at[d], dsend.at[which, k - 1], drecv.at[which, d], at_dp(t))
            c.start()
            pending.append(c)

    def from_dp(which, dst):
        for k in range(1, groups):
            f = lax.rem(d + k, groups)
            slot = dst.at[f]
            send(slot, slot, dsend.at[which, 0], drecv.at[which, f], at_dp(f)).wait_recv()

    to_mp(0, lambda t: dots_out.at[t], dots_in)
    squares = normed * normed
    ones = jnp.ones((8, block), F32)
    high = lax.Precision.HIGHEST
    sq_row = jnp.concatenate(
        [matmul(ones, squares[0], 1, 1, high), matmul(ones, squares[1], 1, 1, high)], axis=1
    )
    sq_in[m] = sq_row[:1]
    to_mp(1, lambda t: sq_in.at[m], sq_in)

    mine = pl.ds(pl.multiple_of(m * own_rows, own_rows), own_rows)
    ids = owner[mine, :] * here + local[mine, :]
    column = lax.broadcasted_iota(jnp.int32, (own_rows, pairs), 1)
    row = lax.broadcasted_iota(jnp.int32, (own_rows, pairs), 0) + me * own_rows
    own = (row == column).astype(F32)
    count = jnp.zeros((own_rows, pairs), F32)
    for k in range(ids.shape[1]):
        count = count + (ids[:, k : k + 1] == column).astype(F32)

    from_mp(1, sq_in)
    sq_all[d] = jnp.sum(sq_in[...], axis=0)
    to_dp(0, lambda t: sq_all.at[d], sq_all)
    from_mp(0, dots_in)
    partial_dots = dots_out[m].astype(F32)
    for k in range(1, quarters):
        partial_dots = partial_dots + dots_in[lax.rem(m + k, quarters)].astype(F32)
    half_out[...] = partial_dots.astype(BF)
    to_dp(1, lambda t: half_out.at[t], half_in)
    from_dp(0, sq_all)
    recip = lax.rsqrt(jnp.sum(sq_all[...], axis=0) + EPS)
    scale[...] = jnp.broadcast_to(recip, (block, 2 * pairs)).T
    half_in[d] = half_out[d]
    from_dp(1, half_in)
    recip_q = scale[pl.ds(pl.multiple_of(me * own_rows, own_rows), own_rows), :][:, :1]
    cosine = jnp.sum(half_in[...].astype(F32), axis=0) * recip_q * recip[:, pairs:]
    expo = jnp.exp(cosine / TAU)
    prob = expo / jnp.sum((own + count) * expo, axis=1, keepdims=True)
    wts_neg = LOSS_SCALE * (count * prob) / TAU
    wts_pos = LOSS_SCALE * (own * (prob - 1.0)) / TAU
    along = (wts_neg + wts_pos) * cosine
    along_q = own * jnp.sum(along, axis=1, keepdims=True)
    extra_in[d] = jnp.concatenate(
        [
            jnp.sum(wts_pos, axis=0, keepdims=True),
            jnp.sum(along_q, axis=0, keepdims=True),
            jnp.sum(along, axis=0, keepdims=True),
        ],
        axis=1,
    )
    wts_all[m, d] = wts_neg.astype(BF)
    to_dp(2, lambda t: wts_all.at[m, d], wts_all.at[m])
    to_dp(3, lambda t: extra_in.at[d], extra_in)
    scaled = scale[...].reshape(2, pairs, block)
    unit = normed * scaled
    emb = unit.astype(BF)
    from_dp(2, wts_all.at[m])
    to_mp(2, lambda t: wts_all.at[m], wts_all)
    from_dp(3, extra_in)
    extra_all[m] = jnp.sum(extra_in[...], axis=0)
    to_mp(3, lambda t: extra_all.at[m], extra_all)
    from_mp(3, extra_all)
    extra = jnp.sum(extra_all[...], axis=0)
    extra = jnp.broadcast_to(extra, (block, 3 * pairs)).T
    from_mp(2, wts_all)
    wts = jnp.stack([wts_all[j] for j in range(quarters)], axis=1).reshape(pairs, pairs)
    pos = extra[:pairs]
    grad_q = matmul(wts, emb[1], 1, 0) + pos * emb[1].astype(F32)
    dn_q = scaled[0] * (grad_q - unit[0] * extra[pairs : 2 * pairs])
    here_cols = pl.ds(pl.multiple_of(m * block, block), block)
    dh[0, :, here_cols] = (dn_q * gain_row).astype(BF)

    def dh_slot(half, t):
        return dh.at[half, :, pl.ds(pl.multiple_of(t * block, block), block)]

    def send_dh(half, t, k, dev):
        slot = dh_slot(half, t)
        c = send(slot, slot, hsend.at[half, k], hrecv.at[half, t], at_mp(dev))
        c.start()
        pending.append(c)

    def wait_dh(half, t):
        slot = dh_slot(half, t)
        send(slot, slot, hsend.at[0, 0], hrecv.at[half, t], at_mp(pair)).wait_recv()

    send_dh(0, m, 0, across)
    send_dh(0, m, 1, pair)
    grad_e = matmul(wts, emb[0], 0, 0) + pos * emb[0].astype(F32)
    dn_e = scaled[1] * (grad_e - unit[1] * extra[2 * pairs :])
    dh[1, :, here_cols] = (dn_e * gain_row).astype(BF)
    send_dh(1, m, 0, across)
    send_dh(1, m, 1, pair)
    gg[m, d] = jnp.sum(dn_q * hidden[0] + dn_e * hidden[1], axis=0, keepdims=True)
    to_dp(4, lambda t: gg.at[m, d], gg.at[m])
    for half in range(2):
        wait_dh(half, across)
        send_dh(half, across, 2, pair)
    from_dp(4, gg.at[m])
    to_mp(4, lambda t: gg.at[m], gg)
    for half in range(2):
        wait_dh(half, pair)
        wait_dh(half, pair + across - m)

    def partial(s):
        rows = dh[:, grp(s), :].reshape(2 * here, -1)
        return matmul(rows, w_out[...], 1, 0).reshape(2, here, -1)

    for k in range(depth):
        tz = lax.rem(zc + 1 + k, depth)
        xpart[k] = partial(tz * 2 + (1 - xc)).astype(BF)
        c = send(xpart.at[k], xin.at[k], xsend2.at[k], xrecv2.at[k], at_dp(partner))
        c.start()
        pending.append(c)
    last = None
    for k in range(depth):
        tz = lax.rem(zc + 1 + k, depth)
        value = partial(tz * 2 + xc)
        send(xpart.at[k], xin.at[k], xsend2.at[k], xrecv2.at[k], at_dp(partner)).wait_recv()
        value = value + xin[k].astype(F32)
        if k < depth - 1:
            zpart[k] = value.astype(BF)
            c = send(zpart.at[k], zin.at[k], zsend2.at[k], zrecv2.at[k], at_dp(tz * 2 + xc))
            c.start()
            pending.append(c)
        else:
            last = value
    attn_now = last
    for j in range(quarters):
        cols = pl.ds(j * block, block)
        out = matmul(dh[0, :, cols], rows_a[0], 0, 0) + matmul(dh[1, :, cols], rows_a[1], 0, 0)
        weight_grad[j * block : (j + 1) * block, :] = out
    from_mp(4, gg)
    for a in range(2):
        for j in range(quarters):
            gain_grad[a * quarters + j] = gg[j, 2 * m + a]
    for k in range(depth - 1):
        send(zpart.at[k], zin.at[k], zsend2.at[k], zrecv2.at[k], at_dp(partner)).wait_recv()
        attn_now = attn_now + zin[k].astype(F32)
    attn_grad[...] = attn_now.astype(BF)

    for c in pending:
        c.wait_send()
    for c in passed:

        @pl.when(middle)
        def _(c=c):
            c.wait_send()

    for is_self, c in res_sends:

        @pl.when(jnp.logical_not(is_self))
        def _(c=c):
            c.wait_send()


def by_feature(attn, resid, w_out, gain, neg_owner, neg_local):
    groups, quarters = lax.axis_size("dp"), lax.axis_size("mp")
    total = groups * quarters
    here = attn.shape[1]
    pairs = groups * here
    heads = attn.shape[2]
    block = w_out.shape[0] // quarters
    own_rows = pairs // total
    per = resid.shape[2] // block
    depth = groups // 2
    dma = pltpu.SemaphoreType.DMA
    vmem = pl.BlockSpec(memory_space=pltpu.VMEM)
    attn_grad, weight_grad, gain_grad = pl.pallas_call(
        functools.partial(fused, groups, quarters),
        out_shape=(
            jax.ShapeDtypeStruct(attn.shape, BF),
            jax.ShapeDtypeStruct(w_out.shape, F32),
            jax.ShapeDtypeStruct((per, 1, block), F32),
        ),
        in_specs=[pl.BlockSpec(memory_space=pltpu.HBM)] * 6,
        out_specs=(vmem,) * 3,
        scratch_shapes=[
            pltpu.VMEM(w_out.shape, BF),
            pltpu.VMEM(neg_owner.shape, jnp.int32),
            pltpu.VMEM(neg_local.shape, jnp.int32),
            pltpu.VMEM((2, pairs, heads), BF),
            pltpu.VMEM((2, pairs, block), BF),
            pltpu.VMEM((quarters, per, block), F32),
            pltpu.VMEM((quarters, 2, pairs, block), BF),
            pltpu.VMEM((quarters, 2, pairs, block), BF),
            pltpu.VMEM((quarters, 1, 2 * pairs), F32),
            pltpu.VMEM((groups, 1, 2 * pairs), F32),
            pltpu.VMEM((quarters, groups, own_rows, pairs), BF),
            pltpu.VMEM((quarters, groups, own_rows, pairs), BF),
            pltpu.VMEM((groups, own_rows, pairs), BF),
            pltpu.VMEM((groups, own_rows, pairs), BF),
            pltpu.VMEM((quarters, groups, own_rows, pairs), BF),
            pltpu.VMEM((groups, 1, 3 * pairs), F32),
            pltpu.VMEM((quarters, 1, 3 * pairs), F32),
            pltpu.VMEM((2 * pairs, block), F32),
            pltpu.VMEM((quarters, groups, 1, block), F32),
            pltpu.VMEM((2, pairs, quarters * block), BF),
            pltpu.VMEM((depth, 2, here, heads), BF),
            pltpu.VMEM((depth, 2, here, heads), BF),
            pltpu.VMEM((depth - 1, 2, here, heads), BF),
            pltpu.VMEM((depth - 1, 2, here, heads), BF),
            dma((6,)),
            dma((depth + 1,)),
            dma((depth,)),
            dma((groups,)),
            dma((per,)),
            dma((groups,)),
            dma((quarters - 1,)),
            dma((quarters,)),
            dma((quarters - 1, groups)),
            dma((quarters, groups)),
            dma((5, quarters - 1)),
            dma((5, quarters)),
            dma((5, groups - 1)),
            dma((5, groups)),
            dma((2, 3)),
            dma((2, quarters)),
            dma((depth,)),
            dma((depth,)),
            dma((depth - 1,)),
            dma((depth - 1,)),
        ],
        compiler_params=pltpu.CompilerParams(
            collective_id=0, has_side_effects=True, vmem_limit_bytes=60 * 1024 * 1024
        ),
    )(attn, resid, w_out, gain.reshape(per, block), neg_owner, neg_local)
    return attn_grad, weight_grad, gain_grad.reshape(-1)


def shards(attn, resid, w_out, gain, neg_owner, neg_local):
    groups, quarters = lax.axis_size("dp"), lax.axis_size("mp")
    here = attn.shape[1]
    block = w_out.shape[0] // quarters
    fits = quarters == 4 and groups == 8 and block % 128 == 0 and resid.shape[2] == 2 * quarters * block
    fits = fits and groups * here <= 1024 and here % (16 * quarters) == 0
    plan = by_feature if fits else by_query
    return plan(attn, resid, w_out, gain, neg_owner, neg_local)


def solution(mesh):
    in_specs = (
        P(None, "dp", "mp"),
        P(None, "dp", "mp"),
        P("dp", "mp"),
        P("mp"),
        P("dp", None),
        P("dp", None),
    )
    out_specs = (P(None, "dp", "mp"), P("dp", "mp"), P("mp"))
    return jax.shard_map(shards, mesh=mesh, in_specs=in_specs, out_specs=out_specs, check_vma=False)
```

```python
import functools

import jax
import jax.numpy as jnp
from jax import lax
from jax.experimental import pallas as pl
from jax.experimental.pallas import tpu as pltpu
from jax.sharding import PartitionSpec as P

TAU = 0.05
LOSS_SCALE = 32.0
EPS = 1e-06


def by_query(attn, resid, w_out, gain, neg_owner, neg_local):
    groups = lax.axis_size("dp")
    pairs_here = attn.shape[1]
    feats = resid.shape[2]
    neg_count = neg_owner.shape[1]
    capacity = 2 * pairs_here * neg_count // groups
    rows_a = attn.reshape(2 * pairs_here, attn.shape[2])
    weight_full = lax.all_gather(w_out, "dp", axis=0, tiled=True)
    proj_part = lax.dot_general(
        rows_a, weight_full, (((1,), (1,)), ((), ())), preferred_element_type=jnp.float32
    )
    proj = lax.psum_scatter(proj_part, "mp", scatter_dimension=1, tiled=True)
    hidden = resid.reshape(2 * pairs_here, feats).astype(jnp.float32) + proj
    normed = hidden * gain
    squares = lax.psum(jnp.sum(normed * normed, axis=1), "mp")
    recip = lax.rsqrt(squares + EPS)[:, None]
    emb = (normed * recip).astype(jnp.bfloat16)
    query = emb[:pairs_here]
    docs = emb[pairs_here:]
    flat_owner = neg_owner.reshape(-1)
    flat_local = neg_local.reshape(-1)
    onehot = (flat_owner[:, None] == jnp.arange(groups, dtype=jnp.int32)[None, :]).astype(jnp.int32)
    ranks = jnp.sum((jnp.cumsum(onehot, axis=0) - 1) * onehot, axis=1)
    slot = flat_owner * capacity + ranks
    request = jnp.full((groups * capacity,), -1, jnp.int32).at[slot].set(flat_local)
    asked = lax.all_to_all(
        request.reshape(groups, capacity), "dp", split_axis=0, concat_axis=0, tiled=True
    )
    valid = asked >= 0
    safe_rows = jnp.maximum(asked, 0)
    outgoing = jnp.where(valid[:, :, None], docs[safe_rows], jnp.zeros((), jnp.bfloat16))
    fetched = lax.all_to_all(outgoing, "dp", split_axis=0, concat_axis=0, tiled=True)
    neg_emb = fetched.reshape(groups * capacity, feats)[slot].reshape(pairs_here, neg_count, feats)
    pos_part = jnp.sum(query.astype(jnp.float32) * docs.astype(jnp.float32), axis=1)
    neg_part = jnp.einsum("pd,pkd->pk", query, neg_emb, preferred_element_type=jnp.float32)
    partial_value = jnp.concatenate([pos_part[:, None], neg_part], axis=1)
    scores = lax.psum(partial_value, "mp") / TAU
    expo = jnp.exp(scores)
    prob = expo / jnp.sum(expo, axis=1, keepdims=True)
    first = (jnp.arange(neg_count + 1) == 0).astype(jnp.float32)[None, :]
    wts = LOSS_SCALE * (prob - first) / TAU
    query_f = query.astype(jnp.float32)
    grad_query = wts[:, 0:1] * docs.astype(jnp.float32) + jnp.einsum(
        "pk,pkd->pd", wts[:, 1:], neg_emb, preferred_element_type=jnp.float32
    )
    terms = (wts[:, 1:, None] * query_f[:, None, :]).astype(jnp.bfloat16)
    slot_buffer = (
        jnp.zeros((groups * capacity, feats), jnp.bfloat16).at[slot].set(terms.reshape(-1, feats))
    )
    returned = lax.all_to_all(
        slot_buffer.reshape(groups, capacity, feats), "dp", split_axis=0, concat_axis=0, tiled=True
    )
    targets = jnp.where(valid, asked, pairs_here).reshape(-1)
    selector = (jnp.arange(pairs_here, dtype=jnp.int32)[:, None] == targets[None, :]).astype(
        jnp.bfloat16
    )
    grad_docs = wts[:, 0:1] * query_f + jnp.dot(
        selector, returned.reshape(-1, feats), preferred_element_type=jnp.float32
    )
    demb = jnp.concatenate([grad_query, grad_docs], axis=0)
    inner = lax.psum(jnp.sum(normed * demb, axis=1), "mp")[:, None]
    dnorm = recip * demb - recip * recip * recip * normed * inner
    gain_grad = lax.psum(jnp.sum(dnorm * hidden, axis=0), "dp")
    dh = (dnorm * gain).astype(jnp.bfloat16)
    dh_full = lax.all_gather(dh, "mp", axis=1, tiled=True)
    attn_grad = (
        jnp.dot(dh_full, weight_full, preferred_element_type=jnp.float32)
        .astype(jnp.bfloat16)
        .reshape(attn.shape)
    )
    weight_grad = lax.psum_scatter(
        lax.dot_general(
            dh_full, rows_a, (((0,), (0,)), ((), ())), preferred_element_type=jnp.float32
        ),
        "dp",
        scatter_dimension=0,
        tiled=True,
    )
    return (attn_grad, weight_grad, gain_grad)


MESH = pl.DeviceIdType.MESH
BF = jnp.bfloat16
F32 = jnp.float32


def matmul(left, right, left_dim, right_dim):
    return lax.dot_general(
        left,
        right,
        (((left_dim,), (right_dim,)), ((), ())),
        preferred_element_type=F32,
    )


def fused(
    groups,
    quarters,
    attn,
    resid,
    w_hbm,
    gain,
    owner_hbm,
    local_hbm,
    attn_grad,
    weight_grad,
    gain_grad,
    w_out,
    owner,
    local,
    rows_a,
    res_all,
    gain_all,
    proj_out,
    proj_in,
    sq_in,
    sq_all,
    dots_out,
    dots_in,
    half_out,
    half_in,
    wts_all,
    extra_in,
    extra_all,
    scale,
    gg,
    dh,
    part,
    xpart,
    xin,
    zpart,
    zin,
    load,
    zsend,
    xsend,
    arecv,
    rsend,
    rrecv,
    gsend,
    grecv,
    psend,
    precv,
    msend,
    mrecv,
    dsend,
    drecv,
    hsend,
    hrecv,
    xsend2,
    xrecv2,
    zsend2,
    zrecv2,
):
    d, m = lax.axis_index("dp"), lax.axis_index("mp")
    total = groups * quarters
    me = d * quarters + m
    here = attn.shape[1]
    pairs = groups * here
    block = w_out.shape[0] // quarters
    pair, across = m + 1 - 2 * lax.rem(m, 2), lax.rem(m + 2, quarters)
    own_rows = pairs // total
    zc, xc = d // 2, d % 2
    depth = groups // 2
    partner = zc * 2 + (1 - xc)

    def at_dp(t):
        return (t, m)

    def at_mp(t):
        return (d, t)

    def at_any(t):
        return (t // quarters, t % quarters)

    def send(src, dst, s, r, dev):
        return pltpu.make_async_remote_copy(
            src_ref=src, dst_ref=dst, send_sem=s, recv_sem=r, device_id=dev, device_id_type=MESH
        )

    def grp(s):
        return pl.ds(pl.multiple_of(s * here, here), here)

    def others(k):
        return lax.rem(me + k, total)

    barrier = pltpu.get_barrier_semaphore()

    loads = [
        pltpu.make_async_copy(attn, rows_a.at[:, grp(d), :], load.at[0]),
        pltpu.make_async_copy(w_hbm, w_out, load.at[1]),
        pltpu.make_async_copy(gain, gain_all.at[m], load.at[2]),
        pltpu.make_async_copy(owner_hbm, owner, load.at[3]),
        pltpu.make_async_copy(local_hbm, local, load.at[4]),
    ]
    for c in loads:
        c.start()

    def greet(k, c):
        pl.semaphore_signal(barrier, inc=1, device_id=at_any(others(k)), device_id_type=MESH)
        return c

    lax.fori_loop(1, total, greet, 0)
    pl.semaphore_wait(barrier, total - 1)

    pending = []
    first = send(attn, rows_a.at[:, grp(d), :], xsend.at[0], arecv.at[d], at_dp(partner))
    first.start()
    pending.append(first)
    middle = (zc + 1) // 2 == 1
    near = zc + 1 - 2 * lax.rem(zc, 2)
    c = send(attn, rows_a.at[:, grp(d), :], zsend.at[0], arecv.at[d], at_dp(near * 2 + xc))
    c.start()
    pending.append(c)
    passed = [send(attn, rows_a.at[:, grp(d), :], zsend.at[1], arecv.at[d], at_dp((3 - zc) * 2 + xc))]

    @pl.when(middle)
    def _():
        passed[0].start()

    for k in range(1, quarters):
        c = send(gain, gain_all.at[m], gsend.at[k - 1], grecv.at[m], at_mp(lax.rem(m + k, quarters)))
        c.start()
        pending.append(c)

    res_sends = []
    for a in range(2):
        for j in range(quarters):
            cols = pl.ds((a * quarters + j) * block, block)
            td = 2 * m + a
            is_self = jnp.logical_and(td == d, m == j)
            c = send(
                resid.at[:, :, cols],
                res_all.at[:, grp(d), :],
                rsend.at[a * quarters + j],
                rrecv.at[d],
                (td, jnp.int32(j)),
            )
            res_sends.append((is_self, c))

            @pl.when(jnp.logical_not(is_self))
            def _(c=c):
                c.start()

            @pl.when(is_self)
            def _(cols=cols):
                c = pltpu.make_async_copy(
                    resid.at[:, :, cols], res_all.at[:, grp(d), :], load.at[5]
                )
                c.start()
                c.wait()

    def project(s, i):
        part = matmul(rows_a[:, grp(s), :].reshape(2 * here, -1), w_out[...], 1, 1)
        for j in range(quarters):
            piece = part[:, j * block : (j + 1) * block].astype(BF)
            proj_out[j, :, grp(s), :] = piece.reshape(2, here, block)
        for k in range(1, quarters):
            t = lax.rem(m + k, quarters)
            c = send(
                proj_out.at[t, :, grp(s), :],
                proj_in.at[m, :, grp(s), :],
                psend.at[k - 1, i],
                precv.at[m, s],
                at_mp(t),
            )
            c.start()
            pending.append(c)

    def wait_rows(s):
        send(attn, rows_a.at[:, grp(s), :], zsend.at[0], arecv.at[s], at_dp(partner)).wait_recv()

    loads[0].wait()
    loads[1].wait()
    project(d, 0)
    half = zc // 2
    nearest = (near, 2 - half, 3 - 3 * half)
    for k in range(1, depth):
        s = nearest[k - 1] * 2 + xc
        onward = 3 - zc if k == 1 else 3 * (zc - 1)
        wait_rows(s)
        slot = rows_a.at[:, grp(s), :]
        c = send(slot, slot, zsend.at[k + 1], arecv.at[s], at_dp(onward * 2 + xc))
        passed.append(c)

        @pl.when(middle)
        def _(c=c):
            c.start()

        c = send(slot, slot, xsend.at[k], arecv.at[s], at_dp(partner))
        c.start()
        pending.append(c)
        project(s, k)
    for k in range(depth):
        s = (zc if k == 0 else nearest[k - 1]) * 2 + (1 - xc)
        wait_rows(s)
        project(s, depth + k)

    for c in loads[2:]:
        c.wait()
    for k in range(1, quarters):
        f = lax.rem(m + k, quarters)
        send(gain, gain_all.at[f], gsend.at[0], grecv.at[f], at_mp(f)).wait_recv()
    source = d // 2
    for s in range(groups):

        @pl.when(jnp.logical_not(jnp.logical_and(source == m, d == s)))
        def _(s=s):
            send(
                resid.at[:, :, pl.ds(0, block)],
                res_all.at[:, grp(s), :],
                rsend.at[0],
                rrecv.at[s],
                at_dp(partner),
            ).wait_recv()

    for k in range(1, quarters):
        f = lax.rem(m + k, quarters)
        for s in range(groups):
            slot = proj_in.at[f, :, grp(s), :]
            send(slot, slot, psend.at[0, 0], precv.at[f, s], at_mp(f)).wait_recv()

    proj = proj_out[m].astype(F32)
    for k in range(1, quarters):
        proj = proj + proj_in[lax.rem(m + k, quarters)].astype(F32)
    hidden = res_all[...].astype(F32) + proj
    gain_row = gain_all[source, pl.ds(lax.rem(d, 2) * quarters + m, 1), :]
    normed = hidden * gain_row
    rough = normed.astype(BF)
    dots = matmul(rough[0], rough[1], 1, 1).astype(BF)
    dots = dots.reshape(groups, quarters, own_rows, pairs)
    for j in range(quarters):
        dots_out[j] = dots[:, j]

    def to_mp(which, src, dst):
        for k in range(1, quarters):
            t = lax.rem(m + k, quarters)
            c = send(src(t), dst.at[m], msend.at[which, k - 1], mrecv.at[which, m], at_mp(t))
            c.start()
            pending.append(c)

    def from_mp(which, dst):
        for k in range(1, quarters):
            f = lax.rem(m + k, quarters)
            slot = dst.at[f]
            send(slot, slot, msend.at[which, 0], mrecv.at[which, f], at_mp(f)).wait_recv()

    def to_dp(which, src, dst):
        for k in range(1, groups):
            t = lax.rem(d + k, groups)
            c = send(src(t), dst.at[d], dsend.at[which, k - 1], drecv.at[which, d], at_dp(t))
            c.start()
            pending.append(c)

    def from_dp(which, dst):
        for k in range(1, groups):
            f = lax.rem(d + k, groups)
            slot = dst.at[f]
            send(slot, slot, dsend.at[which, 0], drecv.at[which, f], at_dp(f)).wait_recv()

    to_mp(0, lambda t: dots_out.at[t], dots_in)
    squares = normed * normed
    ones = jnp.ones((16, block), BF)
    upper = squares.astype(BF)
    lower = (squares - upper.astype(F32)).astype(BF)
    sq_row = jnp.concatenate(
        [matmul(ones, upper[h], 1, 1) + matmul(ones, lower[h], 1, 1) for h in range(2)], axis=1
    )
    sq_in[m] = sq_row[:1]
    to_mp(1, lambda t: sq_in.at[m], sq_in)

    mine = pl.ds(pl.multiple_of(m * own_rows, own_rows), own_rows)
    ids = owner[mine, :] * here + local[mine, :]
    column = lax.broadcasted_iota(jnp.int32, (own_rows, pairs), 1)
    row = lax.broadcasted_iota(jnp.int32, (own_rows, pairs), 0) + me * own_rows
    own = (row == column).astype(F32)
    count = jnp.zeros((own_rows, pairs), F32)
    for k in range(ids.shape[1]):
        count = count + (ids[:, k : k + 1] == column).astype(F32)

    from_mp(1, sq_in)
    sq_all[d] = jnp.sum(sq_in[...], axis=0)
    to_dp(0, lambda t: sq_all.at[d], sq_all)
    from_mp(0, dots_in)
    partial_dots = dots_out[m].astype(F32)
    for k in range(1, quarters):
        partial_dots = partial_dots + dots_in[lax.rem(m + k, quarters)].astype(F32)
    half_out[...] = partial_dots.astype(BF)
    to_dp(1, lambda t: half_out.at[t], half_in)
    from_dp(0, sq_all)
    recip = lax.rsqrt(jnp.sum(sq_all[...], axis=0) + EPS)
    scale[...] = jnp.broadcast_to(recip, (block, 2 * pairs)).T
    half_in[d] = half_out[d]
    from_dp(1, half_in)
    recip_q = scale[pl.ds(pl.multiple_of(me * own_rows, own_rows), own_rows), :][:, :1]
    cosine = jnp.sum(half_in[...].astype(F32), axis=0) * recip_q * recip[:, pairs:]
    expo = jnp.exp(cosine / TAU)
    prob = expo / jnp.sum((own + count) * expo, axis=1, keepdims=True)
    wts_neg = LOSS_SCALE * (count * prob) / TAU
    wts_pos = LOSS_SCALE * (own * (prob - 1.0)) / TAU
    along = (wts_neg + wts_pos) * cosine
    along_q = own * jnp.sum(along, axis=1, keepdims=True)
    extra_in[d] = jnp.concatenate(
        [
            jnp.sum(wts_pos, axis=0, keepdims=True),
            jnp.sum(along_q, axis=0, keepdims=True),
            jnp.sum(along, axis=0, keepdims=True),
        ],
        axis=1,
    )
    wts_all[m, d] = wts_neg.astype(BF)
    to_dp(2, lambda t: wts_all.at[m, d], wts_all.at[m])
    to_dp(3, lambda t: extra_in.at[d], extra_in)
    scaled = scale[...].reshape(2, pairs, block)
    unit = normed * scaled
    emb = unit.astype(BF)
    from_dp(2, wts_all.at[m])
    to_mp(2, lambda t: wts_all.at[m], wts_all)
    from_dp(3, extra_in)
    extra_all[m] = jnp.sum(extra_in[...], axis=0)
    to_mp(3, lambda t: extra_all.at[m], extra_all)
    from_mp(3, extra_all)
    extra = jnp.sum(extra_all[...], axis=0)
    extra = jnp.broadcast_to(extra, (block, 3 * pairs)).T
    from_mp(2, wts_all)
    wts = jnp.stack([wts_all[j] for j in range(quarters)], axis=1).reshape(pairs, pairs)
    pos = extra[:pairs]
    grad_q = matmul(wts, emb[1], 1, 0) + pos * emb[1].astype(F32)
    dn_q = scaled[0] * (grad_q - unit[0] * extra[pairs : 2 * pairs])
    here_cols = pl.ds(pl.multiple_of(m * block, block), block)
    dh[0, :, here_cols] = (dn_q * gain_row).astype(BF)

    def dh_slot(half, t):
        return dh.at[half, :, pl.ds(pl.multiple_of(t * block, block), block)]

    def send_dh(half, t, k, dev):
        slot = dh_slot(half, t)
        c = send(slot, slot, hsend.at[half, k], hrecv.at[half, t], at_mp(dev))
        c.start()
        pending.append(c)

    def wait_dh(half, t):
        slot = dh_slot(half, t)
        send(slot, slot, hsend.at[0, 0], hrecv.at[half, t], at_mp(pair)).wait_recv()

    send_dh(0, m, 0, across)
    send_dh(0, m, 1, pair)
    grad_e = matmul(wts, emb[0], 0, 0) + pos * emb[0].astype(F32)
    dn_e = scaled[1] * (grad_e - unit[1] * extra[2 * pairs :])
    dh[1, :, here_cols] = (dn_e * gain_row).astype(BF)
    send_dh(1, m, 0, across)
    send_dh(1, m, 1, pair)
    gg[m, d] = jnp.sum(dn_q * hidden[0] + dn_e * hidden[1], axis=0, keepdims=True)
    to_dp(4, lambda t: gg.at[m, d], gg.at[m])
    order = [lax.rem(zc + 1 + k, depth) for k in range(depth)]

    def x_copy(half, k):
        slot = (half, order[k])
        return send(
            xpart.at[slot], xin.at[slot], xsend2.at[slot], xrecv2.at[slot], at_dp(partner)
        )

    def z_copy(half, k):
        slot = (half, k)
        dev = at_dp(order[k] * 2 + xc)
        return send(zpart.at[slot], zin.at[slot], zsend2.at[slot], zrecv2.at[slot], dev)

    for half in range(2):
        wait_dh(half, across)
        send_dh(half, across, 2, pair)
        wait_dh(half, pair)
        wait_dh(half, pair + across - m)
        part[half] = matmul(dh[half], w_out[...], 1, 0).reshape(depth, 2, here, -1)
        xpart[half] = part[half, :, 1 - xc].astype(BF)
        for k in range(depth):
            c = x_copy(half, k)
            c.start()
            pending.append(c)
    from_dp(4, gg.at[m])
    to_mp(4, lambda t: gg.at[m], gg)
    weight_grad[...] = matmul(dh[0], rows_a[0], 0, 0)
    attn_now = []
    for half in range(2):
        for k in range(depth):
            x_copy(half, k).wait_recv()
            value = part[half, order[k], xc] + xin[half, order[k]].astype(F32)
            if k < depth - 1:
                zpart[half, k] = value.astype(BF)
                c = z_copy(half, k)
                c.start()
                pending.append(c)
            else:
                attn_now.append(value)
    weight_grad[...] += matmul(dh[1], rows_a[1], 0, 0)
    from_mp(4, gg)
    for a in range(2):
        for j in range(quarters):
            gain_grad[a * quarters + j] = gg[j, 2 * m + a]
    for half in range(2):
        value = attn_now[half]
        for k in range(depth - 1):
            z_copy(half, k).wait_recv()
            value = value + zin[half, k].astype(F32)
        attn_grad[half] = value.astype(BF)

    for c in pending:
        c.wait_send()
    for c in passed:

        @pl.when(middle)
        def _(c=c):
            c.wait_send()

    for is_self, c in res_sends:

        @pl.when(jnp.logical_not(is_self))
        def _(c=c):
            c.wait_send()


def by_feature(attn, resid, w_out, gain, neg_owner, neg_local):
    groups, quarters = lax.axis_size("dp"), lax.axis_size("mp")
    total = groups * quarters
    here = attn.shape[1]
    pairs = groups * here
    heads = attn.shape[2]
    block = w_out.shape[0] // quarters
    own_rows = pairs // total
    per = resid.shape[2] // block
    depth = groups // 2
    dma = pltpu.SemaphoreType.DMA
    vmem = pl.BlockSpec(memory_space=pltpu.VMEM)
    attn_grad, weight_grad, gain_grad = pl.pallas_call(
        functools.partial(fused, groups, quarters),
        out_shape=(
            jax.ShapeDtypeStruct(attn.shape, BF),
            jax.ShapeDtypeStruct(w_out.shape, F32),
            jax.ShapeDtypeStruct((per, 1, block), F32),
        ),
        in_specs=[pl.BlockSpec(memory_space=pltpu.HBM)] * 6,
        out_specs=(vmem,) * 3,
        scratch_shapes=[
            pltpu.VMEM(w_out.shape, BF),
            pltpu.VMEM(neg_owner.shape, jnp.int32),
            pltpu.VMEM(neg_local.shape, jnp.int32),
            pltpu.VMEM((2, pairs, heads), BF),
            pltpu.VMEM((2, pairs, block), BF),
            pltpu.VMEM((quarters, per, block), F32),
            pltpu.VMEM((quarters, 2, pairs, block), BF),
            pltpu.VMEM((quarters, 2, pairs, block), BF),
            pltpu.VMEM((quarters, 1, 2 * pairs), F32),
            pltpu.VMEM((groups, 1, 2 * pairs), F32),
            pltpu.VMEM((quarters, groups, own_rows, pairs), BF),
            pltpu.VMEM((quarters, groups, own_rows, pairs), BF),
            pltpu.VMEM((groups, own_rows, pairs), BF),
            pltpu.VMEM((groups, own_rows, pairs), BF),
            pltpu.VMEM((quarters, groups, own_rows, pairs), BF),
            pltpu.VMEM((groups, 1, 3 * pairs), F32),
            pltpu.VMEM((quarters, 1, 3 * pairs), F32),
            pltpu.VMEM((2 * pairs, block), F32),
            pltpu.VMEM((quarters, groups, 1, block), F32),
            pltpu.VMEM((2, pairs, quarters * block), BF),
            pltpu.VMEM((2, depth, 2, here, heads), F32),
            pltpu.VMEM((2, depth, here, heads), BF),
            pltpu.VMEM((2, depth, here, heads), BF),
            pltpu.VMEM((2, depth - 1, here, heads), BF),
            pltpu.VMEM((2, depth - 1, here, heads), BF),
            dma((6,)),
            dma((depth + 1,)),
            dma((depth,)),
            dma((groups,)),
            dma((per,)),
            dma((groups,)),
            dma((quarters - 1,)),
            dma((quarters,)),
            dma((quarters - 1, groups)),
            dma((quarters, groups)),
            dma((5, quarters - 1)),
            dma((5, quarters)),
            dma((5, groups - 1)),
            dma((5, groups)),
            dma((2, 3)),
            dma((2, quarters)),
            dma((2, depth)),
            dma((2, depth)),
            dma((2, depth - 1)),
            dma((2, depth - 1)),
        ],
        compiler_params=pltpu.CompilerParams(
            collective_id=0, has_side_effects=True, vmem_limit_bytes=48 * 1024 * 1024
        ),
    )(attn, resid, w_out, gain.reshape(per, block), neg_owner, neg_local)
    return attn_grad, weight_grad, gain_grad.reshape(-1)


def shards(attn, resid, w_out, gain, neg_owner, neg_local):
    groups, quarters = lax.axis_size("dp"), lax.axis_size("mp")
    here = attn.shape[1]
    block = w_out.shape[0] // quarters
    fits = quarters == 4 and groups == 8 and block % 128 == 0 and resid.shape[2] == 2 * quarters * block
    fits = fits and groups * here <= 1024 and here % (16 * quarters) == 0
    plan = by_feature if fits else by_query
    return plan(attn, resid, w_out, gain, neg_owner, neg_local)


def solution(mesh):
    in_specs = (
        P(None, "dp", "mp"),
        P(None, "dp", "mp"),
        P("dp", "mp"),
        P("mp"),
        P("dp", None),
        P("dp", None),
    )
    out_specs = (P(None, "dp", "mp"), P("dp", "mp"), P("mp"))
    return jax.shard_map(shards, mesh=mesh, in_specs=in_specs, out_specs=out_specs, check_vma=False)
```

```python
import functools

import jax
import jax.numpy as jnp
from jax import lax
from jax.experimental import pallas as pl
from jax.experimental.pallas import tpu as pltpu
from jax.sharding import PartitionSpec as P

TAU = 0.05
LOSS_SCALE = 32.0
EPS = 1e-06


def by_query(attn, resid, w_out, gain, neg_owner, neg_local):
    groups = lax.axis_size("dp")
    pairs_here = attn.shape[1]
    feats = resid.shape[2]
    neg_count = neg_owner.shape[1]
    capacity = 2 * pairs_here * neg_count // groups
    rows_a = attn.reshape(2 * pairs_here, attn.shape[2])
    weight_full = lax.all_gather(w_out, "dp", axis=0, tiled=True)
    proj_part = lax.dot_general(
        rows_a, weight_full, (((1,), (1,)), ((), ())), preferred_element_type=jnp.float32
    )
    proj = lax.psum_scatter(proj_part, "mp", scatter_dimension=1, tiled=True)
    hidden = resid.reshape(2 * pairs_here, feats).astype(jnp.float32) + proj
    normed = hidden * gain
    squares = lax.psum(jnp.sum(normed * normed, axis=1), "mp")
    recip = lax.rsqrt(squares + EPS)[:, None]
    emb = (normed * recip).astype(jnp.bfloat16)
    query = emb[:pairs_here]
    docs = emb[pairs_here:]
    flat_owner = neg_owner.reshape(-1)
    flat_local = neg_local.reshape(-1)
    onehot = (flat_owner[:, None] == jnp.arange(groups, dtype=jnp.int32)[None, :]).astype(jnp.int32)
    ranks = jnp.sum((jnp.cumsum(onehot, axis=0) - 1) * onehot, axis=1)
    slot = flat_owner * capacity + ranks
    request = jnp.full((groups * capacity,), -1, jnp.int32).at[slot].set(flat_local)
    asked = lax.all_to_all(
        request.reshape(groups, capacity), "dp", split_axis=0, concat_axis=0, tiled=True
    )
    valid = asked >= 0
    safe_rows = jnp.maximum(asked, 0)
    outgoing = jnp.where(valid[:, :, None], docs[safe_rows], jnp.zeros((), jnp.bfloat16))
    fetched = lax.all_to_all(outgoing, "dp", split_axis=0, concat_axis=0, tiled=True)
    neg_emb = fetched.reshape(groups * capacity, feats)[slot].reshape(pairs_here, neg_count, feats)
    pos_part = jnp.sum(query.astype(jnp.float32) * docs.astype(jnp.float32), axis=1)
    neg_part = jnp.einsum("pd,pkd->pk", query, neg_emb, preferred_element_type=jnp.float32)
    partial_value = jnp.concatenate([pos_part[:, None], neg_part], axis=1)
    scores = lax.psum(partial_value, "mp") / TAU
    expo = jnp.exp(scores)
    prob = expo / jnp.sum(expo, axis=1, keepdims=True)
    first = (jnp.arange(neg_count + 1) == 0).astype(jnp.float32)[None, :]
    wts = LOSS_SCALE * (prob - first) / TAU
    query_f = query.astype(jnp.float32)
    grad_query = wts[:, 0:1] * docs.astype(jnp.float32) + jnp.einsum(
        "pk,pkd->pd", wts[:, 1:], neg_emb, preferred_element_type=jnp.float32
    )
    terms = (wts[:, 1:, None] * query_f[:, None, :]).astype(jnp.bfloat16)
    slot_buffer = (
        jnp.zeros((groups * capacity, feats), jnp.bfloat16).at[slot].set(terms.reshape(-1, feats))
    )
    returned = lax.all_to_all(
        slot_buffer.reshape(groups, capacity, feats), "dp", split_axis=0, concat_axis=0, tiled=True
    )
    targets = jnp.where(valid, asked, pairs_here).reshape(-1)
    selector = (jnp.arange(pairs_here, dtype=jnp.int32)[:, None] == targets[None, :]).astype(
        jnp.bfloat16
    )
    grad_docs = wts[:, 0:1] * query_f + jnp.dot(
        selector, returned.reshape(-1, feats), preferred_element_type=jnp.float32
    )
    demb = jnp.concatenate([grad_query, grad_docs], axis=0)
    inner = lax.psum(jnp.sum(normed * demb, axis=1), "mp")[:, None]
    dnorm = recip * demb - recip * recip * recip * normed * inner
    gain_grad = lax.psum(jnp.sum(dnorm * hidden, axis=0), "dp")
    dh = (dnorm * gain).astype(jnp.bfloat16)
    dh_full = lax.all_gather(dh, "mp", axis=1, tiled=True)
    attn_grad = (
        jnp.dot(dh_full, weight_full, preferred_element_type=jnp.float32)
        .astype(jnp.bfloat16)
        .reshape(attn.shape)
    )
    weight_grad = lax.psum_scatter(
        lax.dot_general(
            dh_full, rows_a, (((0,), (0,)), ((), ())), preferred_element_type=jnp.float32
        ),
        "dp",
        scatter_dimension=0,
        tiled=True,
    )
    return (attn_grad, weight_grad, gain_grad)


MESH = pl.DeviceIdType.MESH
BF = jnp.bfloat16
F32 = jnp.float32


def matmul(left, right, left_dim, right_dim):
    return lax.dot_general(
        left,
        right,
        (((left_dim,), (right_dim,)), ((), ())),
        preferred_element_type=F32,
    )


def fused(
    groups,
    quarters,
    attn,
    resid,
    w_hbm,
    gain,
    ids_hbm,
    attn_grad,
    weight_grad,
    gain_grad,
    w_out,
    ids_here,
    rows_a,
    res_all,
    gain_all,
    proj_out,
    proj_in,
    sq_in,
    sq_all,
    dots_out,
    dots_in,
    half_out,
    half_in,
    wts_all,
    extra_in,
    extra_all,
    scale,
    gg,
    dh,
    part,
    xpart,
    xin,
    zpart,
    zin,
    load,
    zsend,
    xsend,
    arecv,
    rsend,
    rrecv,
    gsend,
    grecv,
    psend,
    precv,
    msend,
    mrecv,
    dsend,
    drecv,
    hsend,
    hrecv,
    xsend2,
    xrecv2,
    zsend2,
    zrecv2,
):
    d, m = lax.axis_index("dp"), lax.axis_index("mp")
    total = groups * quarters
    me = d * quarters + m
    here = attn.shape[1]
    pairs = groups * here
    block = w_out.shape[0] // quarters
    pair, across = m + 1 - 2 * lax.rem(m, 2), lax.rem(m + 2, quarters)
    own_rows = pairs // total
    zc, xc = d // 2, d % 2
    depth = groups // 2
    partner = zc * 2 + (1 - xc)

    def at_dp(t):
        return (t, m)

    def at_mp(t):
        return (d, t)

    def at_any(t):
        return (t // quarters, t % quarters)

    def send(src, dst, s, r, dev):
        return pltpu.make_async_remote_copy(
            src_ref=src, dst_ref=dst, send_sem=s, recv_sem=r, device_id=dev, device_id_type=MESH
        )

    def grp(s):
        return pl.ds(pl.multiple_of(s * here, here), here)

    def others(k):
        return lax.rem(me + k, total)

    barrier = pltpu.get_barrier_semaphore()

    loads = [
        pltpu.make_async_copy(attn, rows_a.at[:, grp(d), :], load.at[0]),
        pltpu.make_async_copy(w_hbm, w_out, load.at[1]),
        pltpu.make_async_copy(gain, gain_all.at[m], load.at[2]),
        pltpu.make_async_copy(ids_hbm, ids_here, load.at[3]),
    ]
    for c in loads:
        c.start()

    def greet(k, c):
        pl.semaphore_signal(barrier, inc=1, device_id=at_any(others(k)), device_id_type=MESH)
        return c

    lax.fori_loop(1, total, greet, 0)
    pl.semaphore_wait(barrier, total - 1)

    pending = []
    first = send(attn, rows_a.at[:, grp(d), :], xsend.at[0], arecv.at[d], at_dp(partner))
    first.start()
    pending.append(first)
    middle = (zc + 1) // 2 == 1
    near = zc + 1 - 2 * lax.rem(zc, 2)
    c = send(attn, rows_a.at[:, grp(d), :], zsend.at[0], arecv.at[d], at_dp(near * 2 + xc))
    c.start()
    pending.append(c)
    passed = [send(attn, rows_a.at[:, grp(d), :], zsend.at[1], arecv.at[d], at_dp((3 - zc) * 2 + xc))]

    @pl.when(middle)
    def _():
        passed[0].start()

    for k in range(1, quarters):
        c = send(gain, gain_all.at[m], gsend.at[k - 1], grecv.at[m], at_mp(lax.rem(m + k, quarters)))
        c.start()
        pending.append(c)

    res_sends = []
    for a in range(2):
        for j in range(quarters):
            cols = pl.ds((a * quarters + j) * block, block)
            td = 2 * m + a
            is_self = jnp.logical_and(td == d, m == j)
            c = send(
                resid.at[:, :, cols],
                res_all.at[:, grp(d), :],
                rsend.at[a * quarters + j],
                rrecv.at[d],
                (td, jnp.int32(j)),
            )
            res_sends.append((is_self, c))

            @pl.when(jnp.logical_not(is_self))
            def _(c=c):
                c.start()

            @pl.when(is_self)
            def _(cols=cols):
                c = pltpu.make_async_copy(
                    resid.at[:, :, cols], res_all.at[:, grp(d), :], load.at[5]
                )
                c.start()
                c.wait()

    def project(s, i):
        part = matmul(rows_a[:, grp(s), :].reshape(2 * here, -1), w_out[...], 1, 1)
        for j in range(quarters):
            piece = part[:, j * block : (j + 1) * block].astype(BF)
            proj_out[j, :, grp(s), :] = piece.reshape(2, here, block)
        for k in range(1, quarters):
            t = lax.rem(m + k, quarters)
            c = send(
                proj_out.at[t, :, grp(s), :],
                proj_in.at[m, :, grp(s), :],
                psend.at[k - 1, i],
                precv.at[m, s],
                at_mp(t),
            )
            c.start()
            pending.append(c)

    def wait_rows(s):
        send(attn, rows_a.at[:, grp(s), :], zsend.at[0], arecv.at[s], at_dp(partner)).wait_recv()

    loads[0].wait()
    loads[1].wait()
    project(d, 0)
    half = zc // 2
    nearest = (near, 2 - half, 3 - 3 * half)
    for k in range(1, depth):
        s = nearest[k - 1] * 2 + xc
        onward = 3 - zc if k == 1 else 3 * (zc - 1)
        wait_rows(s)
        slot = rows_a.at[:, grp(s), :]
        c = send(slot, slot, zsend.at[k + 1], arecv.at[s], at_dp(onward * 2 + xc))
        passed.append(c)

        @pl.when(middle)
        def _(c=c):
            c.start()

        c = send(slot, slot, xsend.at[k], arecv.at[s], at_dp(partner))
        c.start()
        pending.append(c)
        project(s, k)
    for k in range(depth):
        s = (zc if k == 0 else nearest[k - 1]) * 2 + (1 - xc)
        wait_rows(s)
        project(s, depth + k)

    for c in loads[2:]:
        c.wait()
    for k in range(1, quarters):
        f = lax.rem(m + k, quarters)
        send(gain, gain_all.at[f], gsend.at[0], grecv.at[f], at_mp(f)).wait_recv()
    source = d // 2
    for s in range(groups):

        @pl.when(jnp.logical_not(jnp.logical_and(source == m, d == s)))
        def _(s=s):
            send(
                resid.at[:, :, pl.ds(0, block)],
                res_all.at[:, grp(s), :],
                rsend.at[0],
                rrecv.at[s],
                at_dp(partner),
            ).wait_recv()

    for k in range(1, quarters):
        f = lax.rem(m + k, quarters)
        for s in range(groups):
            slot = proj_in.at[f, :, grp(s), :]
            send(slot, slot, psend.at[0, 0], precv.at[f, s], at_mp(f)).wait_recv()

    proj = proj_out[m].astype(F32)
    for k in range(1, quarters):
        proj = proj + proj_in[lax.rem(m + k, quarters)].astype(F32)
    hidden = res_all[...].astype(F32) + proj
    gain_row = gain_all[source, pl.ds(lax.rem(d, 2) * quarters + m, 1), :]
    normed = hidden * gain_row
    rough = normed.astype(BF)
    dots = matmul(rough[0], rough[1], 1, 1).astype(BF)
    dots = dots.reshape(groups, quarters, own_rows, pairs)
    for j in range(quarters):
        dots_out[j] = dots[:, j]

    def to_mp(which, src, dst):
        for k in range(1, quarters):
            t = lax.rem(m + k, quarters)
            c = send(src(t), dst.at[m], msend.at[which, k - 1], mrecv.at[which, m], at_mp(t))
            c.start()
            pending.append(c)

    def from_mp(which, dst):
        for k in range(1, quarters):
            f = lax.rem(m + k, quarters)
            slot = dst.at[f]
            send(slot, slot, msend.at[which, 0], mrecv.at[which, f], at_mp(f)).wait_recv()

    def to_dp(which, src, dst):
        for k in range(1, groups):
            t = lax.rem(d + k, groups)
            c = send(src(t), dst.at[d], dsend.at[which, k - 1], drecv.at[which, d], at_dp(t))
            c.start()
            pending.append(c)

    def from_dp(which, dst):
        for k in range(1, groups):
            f = lax.rem(d + k, groups)
            slot = dst.at[f]
            send(slot, slot, dsend.at[which, 0], drecv.at[which, f], at_dp(f)).wait_recv()

    to_mp(0, lambda t: dots_out.at[t], dots_in)
    squares = normed * normed
    ones = jnp.ones((16, block), BF)
    upper = squares.astype(BF)
    lower = (squares - upper.astype(F32)).astype(BF)
    sq_row = jnp.concatenate(
        [matmul(ones, upper[h], 1, 1) + matmul(ones, lower[h], 1, 1) for h in range(2)], axis=1
    )
    sq_in[m] = sq_row[:1]
    to_mp(1, lambda t: sq_in.at[m], sq_in)

    mine = pl.ds(pl.multiple_of(m * own_rows, own_rows), own_rows)
    ids = ids_here[mine, :]
    column = lax.broadcasted_iota(jnp.int32, (own_rows, pairs), 1)
    row = lax.broadcasted_iota(jnp.int32, (own_rows, pairs), 0) + me * own_rows
    own = (row == column).astype(F32)
    count = jnp.zeros((own_rows, pairs), F32)
    for k in range(ids.shape[1]):
        count = count + (ids[:, k : k + 1] == column).astype(F32)

    from_mp(1, sq_in)
    sq_all[d] = jnp.sum(sq_in[...], axis=0)
    to_dp(0, lambda t: sq_all.at[d], sq_all)
    from_mp(0, dots_in)
    partial_dots = dots_out[m].astype(F32)
    for k in range(1, quarters):
        partial_dots = partial_dots + dots_in[lax.rem(m + k, quarters)].astype(F32)
    half_out[...] = partial_dots.astype(BF)
    to_dp(1, lambda t: half_out.at[t], half_in)
    from_dp(0, sq_all)
    recip = lax.rsqrt(jnp.sum(sq_all[...], axis=0) + EPS)
    scale[...] = jnp.broadcast_to(recip, (block, 2 * pairs)).T
    half_in[d] = half_out[d]
    from_dp(1, half_in)
    recip_q = scale[pl.ds(pl.multiple_of(me * own_rows, own_rows), own_rows), :][:, :1]
    cosine = jnp.sum(half_in[...].astype(F32), axis=0) * recip_q * recip[:, pairs:]
    expo = jnp.exp(cosine / TAU)
    prob = expo / jnp.sum((own + count) * expo, axis=1, keepdims=True)
    wts_neg = LOSS_SCALE * (count * prob) / TAU
    wts_pos = LOSS_SCALE * (own * (prob - 1.0)) / TAU
    along = (wts_neg + wts_pos) * cosine
    along_q = own * jnp.sum(along, axis=1, keepdims=True)
    extra_in[d] = jnp.concatenate(
        [
            jnp.sum(wts_pos, axis=0, keepdims=True),
            jnp.sum(along_q, axis=0, keepdims=True),
            jnp.sum(along, axis=0, keepdims=True),
        ],
        axis=1,
    )
    wts_all[m, d] = wts_neg.astype(BF)
    to_dp(2, lambda t: wts_all.at[m, d], wts_all.at[m])
    to_dp(3, lambda t: extra_in.at[d], extra_in)
    scaled = scale[...].reshape(2, pairs, block)
    unit = normed * scaled
    emb = unit.astype(BF)
    from_dp(2, wts_all.at[m])

    def pass_wts(t, k, dev):
        slot = wts_all.at[t]
        c = send(slot, slot, msend.at[2, k], mrecv.at[2, t], at_mp(dev))
        c.start()
        pending.append(c)

    def wait_wts(t):
        slot = wts_all.at[t]
        send(slot, slot, msend.at[2, 0], mrecv.at[2, t], at_mp(pair)).wait_recv()

    pass_wts(m, 0, across)
    pass_wts(m, 1, pair)
    from_dp(3, extra_in)
    extra_all[m] = jnp.sum(extra_in[...], axis=0)
    to_mp(3, lambda t: extra_all.at[m], extra_all)
    wait_wts(across)
    pass_wts(across, 2, pair)
    from_mp(3, extra_all)
    extra = jnp.sum(extra_all[...], axis=0)
    extra = jnp.broadcast_to(extra, (block, 3 * pairs)).T
    wait_wts(pair)
    wait_wts(pair + across - m)
    wts = jnp.stack([wts_all[j] for j in range(quarters)], axis=1).reshape(pairs, pairs)
    pos = extra[:pairs]
    grad_q = matmul(wts, emb[1], 1, 0) + pos * emb[1].astype(F32)
    dn_q = scaled[0] * (grad_q - unit[0] * extra[pairs : 2 * pairs])
    here_cols = pl.ds(pl.multiple_of(m * block, block), block)
    dh[0, :, here_cols] = (dn_q * gain_row).astype(BF)

    def dh_slot(half, t):
        return dh.at[half, :, pl.ds(pl.multiple_of(t * block, block), block)]

    def send_dh(half, t, k, dev):
        slot = dh_slot(half, t)
        c = send(slot, slot, hsend.at[half, k], hrecv.at[half, t], at_mp(dev))
        c.start()
        pending.append(c)

    def wait_dh(half, t):
        slot = dh_slot(half, t)
        send(slot, slot, hsend.at[0, 0], hrecv.at[half, t], at_mp(pair)).wait_recv()

    send_dh(0, m, 0, across)
    send_dh(0, m, 1, pair)
    grad_e = matmul(wts, emb[0], 0, 0) + pos * emb[0].astype(F32)
    dn_e = scaled[1] * (grad_e - unit[1] * extra[2 * pairs :])
    dh[1, :, here_cols] = (dn_e * gain_row).astype(BF)
    send_dh(1, m, 0, across)
    send_dh(1, m, 1, pair)
    gg[m, d] = jnp.sum(dn_q * hidden[0] + dn_e * hidden[1], axis=0, keepdims=True)
    to_dp(4, lambda t: gg.at[m, d], gg.at[m])
    order = [lax.rem(zc + 1 + k, depth) for k in range(depth)]

    def x_copy(half, k):
        slot = (half, order[k])
        return send(
            xpart.at[slot], xin.at[slot], xsend2.at[slot], xrecv2.at[slot], at_dp(partner)
        )

    def z_copy(half, k):
        slot = (half, k)
        dev = at_dp(order[k] * 2 + xc)
        return send(zpart.at[slot], zin.at[slot], zsend2.at[slot], zrecv2.at[slot], dev)

    for half in range(2):
        wait_dh(half, across)
        send_dh(half, across, 2, pair)
        wait_dh(half, pair)
        wait_dh(half, pair + across - m)
        part[half] = matmul(dh[half], w_out[...], 1, 0).reshape(depth, 2, here, -1)
        xpart[half] = part[half, :, 1 - xc].astype(BF)
        for k in range(depth):
            c = x_copy(half, k)
            c.start()
            pending.append(c)
    from_dp(4, gg.at[m])
    to_mp(4, lambda t: gg.at[m], gg)
    weight_grad[...] = matmul(dh[0], rows_a[0], 0, 0)
    attn_now = []
    for half in range(2):
        for k in range(depth):
            x_copy(half, k).wait_recv()
            value = part[half, order[k], xc] + xin[half, order[k]].astype(F32)
            if k < depth - 1:
                zpart[half, k] = value.astype(BF)
                c = z_copy(half, k)
                c.start()
                pending.append(c)
            else:
                attn_now.append(value)
    weight_grad[...] += matmul(dh[1], rows_a[1], 0, 0)
    from_mp(4, gg)
    for a in range(2):
        for j in range(quarters):
            gain_grad[a * quarters + j] = gg[j, 2 * m + a]
    for half in range(2):
        value = attn_now[half]
        for k in range(depth - 1):
            z_copy(half, k).wait_recv()
            value = value + zin[half, k].astype(F32)
        attn_grad[half] = value.astype(BF)

    for c in pending:
        c.wait_send()
    for c in passed:

        @pl.when(middle)
        def _(c=c):
            c.wait_send()

    for is_self, c in res_sends:

        @pl.when(jnp.logical_not(is_self))
        def _(c=c):
            c.wait_send()


def by_feature(attn, resid, w_out, gain, neg_owner, neg_local):
    groups, quarters = lax.axis_size("dp"), lax.axis_size("mp")
    total = groups * quarters
    here = attn.shape[1]
    pairs = groups * here
    heads = attn.shape[2]
    block = w_out.shape[0] // quarters
    own_rows = pairs // total
    per = resid.shape[2] // block
    depth = groups // 2
    dma = pltpu.SemaphoreType.DMA
    vmem = pl.BlockSpec(memory_space=pltpu.VMEM)
    attn_grad, weight_grad, gain_grad = pl.pallas_call(
        functools.partial(fused, groups, quarters),
        out_shape=(
            jax.ShapeDtypeStruct(attn.shape, BF),
            jax.ShapeDtypeStruct(w_out.shape, F32),
            jax.ShapeDtypeStruct((per, 1, block), F32),
        ),
        in_specs=[pl.BlockSpec(memory_space=pltpu.HBM)] * 5,
        out_specs=(vmem,) * 3,
        scratch_shapes=[
            pltpu.VMEM(w_out.shape, BF),
            pltpu.VMEM(neg_owner.shape, jnp.int32),
            pltpu.VMEM((2, pairs, heads), BF),
            pltpu.VMEM((2, pairs, block), BF),
            pltpu.VMEM((quarters, per, block), F32),
            pltpu.VMEM((quarters, 2, pairs, block), BF),
            pltpu.VMEM((quarters, 2, pairs, block), BF),
            pltpu.VMEM((quarters, 1, 2 * pairs), F32),
            pltpu.VMEM((groups, 1, 2 * pairs), F32),
            pltpu.VMEM((quarters, groups, own_rows, pairs), BF),
            pltpu.VMEM((quarters, groups, own_rows, pairs), BF),
            pltpu.VMEM((groups, own_rows, pairs), BF),
            pltpu.VMEM((groups, own_rows, pairs), BF),
            pltpu.VMEM((quarters, groups, own_rows, pairs), BF),
            pltpu.VMEM((groups, 1, 3 * pairs), F32),
            pltpu.VMEM((quarters, 1, 3 * pairs), F32),
            pltpu.VMEM((2 * pairs, block), F32),
            pltpu.VMEM((quarters, groups, 1, block), F32),
            pltpu.VMEM((2, pairs, quarters * block), BF),
            pltpu.VMEM((2, depth, 2, here, heads), F32),
            pltpu.VMEM((2, depth, here, heads), BF),
            pltpu.VMEM((2, depth, here, heads), BF),
            pltpu.VMEM((2, depth - 1, here, heads), BF),
            pltpu.VMEM((2, depth - 1, here, heads), BF),
            dma((6,)),
            dma((depth + 1,)),
            dma((depth,)),
            dma((groups,)),
            dma((per,)),
            dma((groups,)),
            dma((quarters - 1,)),
            dma((quarters,)),
            dma((quarters - 1, groups)),
            dma((quarters, groups)),
            dma((5, quarters - 1)),
            dma((5, quarters)),
            dma((5, groups - 1)),
            dma((5, groups)),
            dma((2, 3)),
            dma((2, quarters)),
            dma((2, depth)),
            dma((2, depth)),
            dma((2, depth - 1)),
            dma((2, depth - 1)),
        ],
        compiler_params=pltpu.CompilerParams(
            collective_id=0, has_side_effects=True, vmem_limit_bytes=48 * 1024 * 1024
        ),
    )(attn, resid, w_out, gain.reshape(per, block), neg_owner * here + neg_local)
    return attn_grad, weight_grad, gain_grad.reshape(-1)


def shards(attn, resid, w_out, gain, neg_owner, neg_local):
    groups, quarters = lax.axis_size("dp"), lax.axis_size("mp")
    here = attn.shape[1]
    block = w_out.shape[0] // quarters
    fits = quarters == 4 and groups == 8 and block % 128 == 0 and resid.shape[2] == 2 * quarters * block
    fits = fits and groups * here <= 1024 and here % (16 * quarters) == 0
    plan = by_feature if fits else by_query
    return plan(attn, resid, w_out, gain, neg_owner, neg_local)


def solution(mesh):
    in_specs = (
        P(None, "dp", "mp"),
        P(None, "dp", "mp"),
        P("dp", "mp"),
        P("mp"),
        P("dp", None),
        P("dp", None),
    )
    out_specs = (P(None, "dp", "mp"), P("dp", "mp"), P("mp"))
    return jax.shard_map(shards, mesh=mesh, in_specs=in_specs, out_specs=out_specs, check_vma=False)
```
